32 devices in a mesh: groups: 2 (over y), owner: 4 (over z), head: 2 (over x), rep: 2 (over core).
Axes of the slice: x: 2, y: 2, z: 4, core: 2. Of those that a mesh axis runs over, the one named last changes fastest.
Arguments:
- queries: bfloat16 [4096, 8, 512], P(('groups', 'owner', 'rep'), 'head'), parts along dimension 0, may hold values from -10 to 10
- cotangent: bfloat16 [4096, 8, 512], P(('groups', 'owner', 'rep'), 'head'), parts along dimension 0, may hold values from -6 to 6
- own_kv: bfloat16 [4096, 8, 256], P(('groups', 'owner', 'rep'), 'head'), parts along dimension 0, may hold values from -6 to 6
- tables: int32 [4096, 1], P(('groups', 'owner', 'rep')), parts along dimension 0, may hold values from 0 to 3; in each aligned block of 256 rows (0 to 255, 256 to 511, ...) at most 128 rows name the same one
- table_owner: int32 [8], P('groups'), parts along dimension 0, may hold values from 0 to 3, each once
- cache_keys: float32 [8, 8, 1024, 128], P(('groups', 'owner'), 'head', 'rep'), parts along dimension 0, may hold values from -10 to 10
- cache_values: float32 [8, 8, 1024, 128], P(('groups', 'owner'), 'head', 'rep'), parts along dimension 0, may hold values from -6 to 6
- first_moment: float32 [2, 8, 8, 1024, 128], P(None, ('groups', 'owner'), 'head', 'rep'), parts along dimension 1, may hold values from -0.75 to 0.75
- second_moment: float32 [2, 8, 8, 1024, 128], P(None, ('groups', 'owner'), 'head', 'rep'), parts along dimension 1, may hold values from 1e-06 to 0.1
Outputs:
- attended: bfloat16 [4096, 8, 512], P(('groups', 'owner', 'rep'), 'head'), parts along dimension 0
- new_keys: float32 [8, 8, 1024, 128], P(('groups', 'owner'), 'head', 'rep'), parts along dimension 0
- new_values: float32 [8, 8, 1024, 128], P(('groups', 'owner'), 'head', 'rep'), parts along dimension 0
- new_first: float32 [2, 8, 8, 1024, 128], P(None, ('groups', 'owner'), 'head', 'rep'), parts along dimension 1
- new_second: float32 [2, 8, 8, 1024, 128], P(None, ('groups', 'owner'), 'head', 'rep'), parts along dimension 1
The draws below stay inside these ranges and needn't reach their ends.
There are 2 independent parts, one for each index of `groups`. The reference program is written for one: setup_inputs(seed, part) draws one part's arguments, and reference() takes and returns one part's arrays. A program takes and returns all parts, laid end to end along the dimension named above; each array names one. Nothing has to cross between parts.
Inputs may be any that keep to these rules, and one draw needn't show every extreme that they name: `tables`: in the rows of one reader device no table is named by more than 128 tokens, a bound that some block reaches. `table_owner`: each owner holds exactly one table.
All inputs are finite; a program needn't handle non-finite values.
Results may differ from the reference program's by a relative error of at most 0.0085.
Values may be sent and summed in bfloat16 or wider, within the bound.
No kernel may reach another device: no remote copies, remote signals or barrier semaphores. Data moves between devices by JAX's collectives and lax.ppermute only.
A program may use at most 128 MiB of HBM per device.

```python
import math
import jax
import jax.numpy as jnp
import numpy as np
from jax import lax

KVH = 8
GQ = 4
DH = 128
SLOTS = 1024
Q_DEV = 256
CAP = 128
TABLES = 4
ROWS = 2048


def draw_queries(key, part):
    base = jnp.clip(jax.random.normal(key, (ROWS, KVH, GQ * DH), jnp.float32), -6.0, 6.0)
    return base.astype(jnp.bfloat16)


def draw_cache_keys(key, part):
    base = jnp.clip(jax.random.normal(key, (TABLES, KVH, SLOTS, DH), jnp.float32), -6.0, 6.0)
    return base


def steps_of(rng, extent, split, smallest, top_value):
    gain, own = 1.0, jax.random.fold_in(rng, 6)
    for position, blocks in split:
        steps = jnp.exp(jax.random.uniform(jax.random.fold_in(own, position), (blocks,), jnp.float32, smallest / len(split), top_value / len(split)))
        gain = gain * jnp.repeat(steps, extent[position] // blocks).reshape([-1 if axis == position else 1 for axis in range(len(extent))])
    return gain


def shared_out(rng, own, number, rows, number_of, top, reach, skew):
    ranking = jax.random.permutation(rng, number_of)
    heavy_load, usual = portions_of(number_of, rows * top, reach, skew, True), portions_of(number_of, rows * top, reach, skew, False)
    places = jnp.arange(number_of)

    def named(lengths, turn):
        used = int((lengths > 0).sum())
        fixed = max(1, used // 4)
        shifted = fixed + (places - fixed + turn * (used - fixed)) % max(1, number_of - fixed)
        return jnp.zeros((number_of,), jnp.int32).at[ranking[jnp.where(places < fixed, places, shifted)]].set(jnp.asarray(lengths, jnp.int32))

    lengths = jnp.where(number % 4 == 0, named(heavy_load, number // 4), named(usual, number - number // 4 - 1))
    mixed = jax.random.permutation(jax.random.fold_in(own, 3), number_of)
    donor, taker = mixed[0:number_of // 2 * 2:2], mixed[1:number_of // 2 * 2:2]
    margin = jnp.minimum(lengths[donor] - 1, reach - lengths[taker]) // 2
    margin = jnp.where((donor == ranking[0]) | (taker == ranking[0]) | (lengths[taker] == 0), 0, jnp.maximum(margin, 0))
    shifted = jax.random.randint(jax.random.fold_in(own, 4), (number_of // 2,), 0, 1 << 20) % (margin + 1)
    lengths = lengths.at[donor].add(-shifted).at[taker].add(shifted)
    members = jnp.searchsorted(jnp.cumsum(lengths), jnp.arange(rows * top), side="right").astype(jnp.int32)
    table = members.reshape(top, rows).T
    table = table[jax.random.permutation(jax.random.fold_in(own, 1), rows)]
    turn = jax.random.randint(jax.random.fold_in(own, 2), (rows, 1), 0, top)
    return jnp.take_along_axis(table, (jnp.arange(top)[None, :] + turn) % top, axis=1)


def portions_of(amount, total, reach, slope, full):
    weights = [(1 << 20) // math.isqrt(grade ** slope) + 1 for grade in range(1, amount + 1)]
    largest = reach if full else min(reach, max(-(-total // amount), total * weights[0] // sum(weights)))
    least = 1 if total - largest >= amount - 1 else 0
    given, surplus = [largest] + [least] * (amount - 1), total - largest - least * (amount - 1)
    while surplus > 0:
        candidates = [i for i in range(1, amount) if given[i] < largest] or [i for i in range(1, amount) if given[i] < reach]
        mass, left = sum([weights[i] for i in candidates]), surplus
        for i in candidates:
            extra = min(reach - given[i], max(1, left * weights[i] // mass), surplus)
            given[i] = given[i] + extra
            surplus = surplus - extra
    return np.array(given)


def centred(rng, dims, spread, most, split=(), kind=jnp.bfloat16):
    result = jax.random.normal(rng, dims, jnp.float32) * spread
    if len(split) > 0:
        result = steps_of(rng, dims, split, -0.22, 0.18) * result
    return jnp.clip(result, min=-most, max=most).astype(kind)


def setup_inputs(seed: int = 0, part: int = 0) -> dict:
    seeds = jax.random.split(jax.random.key(seed), 10)
    part_splits = jax.random.split(jax.random.fold_in(seeds[9], part), 10)
    queries = draw_queries(jax.random.fold_in(jax.random.fold_in(seeds[9], part), 71), part)
    cotangent = centred(part_splits[1], (ROWS, KVH, GQ * DH), 1.0, 6.0, ((0, 8), (1, 2)))
    own_kv = centred(part_splits[2], (ROWS, KVH, 2 * DH), 1.0, 6.0, ((0, 8), (1, 2)))
    tables_keys = jax.random.split(jax.random.fold_in(part_splits[3], 1), ROWS // Q_DEV)
    tables_turns = jax.random.permutation(jax.random.fold_in(part_splits[3], 3), ROWS // Q_DEV)
    tables = jax.vmap(lambda own, number: shared_out(jax.random.fold_in(part_splits[3], 2), own, number, Q_DEV, TABLES, 1, CAP, 2))(tables_keys, tables_turns).reshape((ROWS, 1))
    table_owner = jax.random.permutation(part_splits[4], TABLES).astype(jnp.int32)
    cache_keys = draw_cache_keys(jax.random.fold_in(jax.random.fold_in(seeds[9], part), 71), part)
    cache_values = centred(part_splits[6], (TABLES, KVH, SLOTS, DH), 1.0, 6.0, ((0, 4), (1, 2), (2, 2)), jnp.float32)
    first_moment = centred(part_splits[7], (2, TABLES, KVH, SLOTS, DH), 0.05, 0.75, ((1, 4), (2, 2), (3, 2)), jnp.float32)
    second_moment = jnp.clip(jnp.exp(math.log(0.1) - 11.512925 * jax.random.uniform(part_splits[8], (2, TABLES, KVH, SLOTS, DH), jnp.float32) ** steps_of(part_splits[8], (2, TABLES, KVH, SLOTS, DH), ((1, 4), (2, 2), (3, 2)), -0.2, 0.2)), 9.999999974752427e-07, 0.1)
    return dict(queries=queries, cotangent=cotangent, own_kv=own_kv, tables=tables, table_owner=table_owner, cache_keys=cache_keys, cache_values=cache_values, first_moment=first_moment, second_moment=second_moment)


def rounded(x):
    return lax.optimization_barrier(x.astype(jnp.bfloat16)).astype(jnp.float32)

def one_owner(args):
    q_rows, c_rows, kv_rows, keys_bf, vals_bf = args
    count = q_rows.shape[0]
    scale = DH ** (-0.5)
    qf = q_rows.astype(jnp.float32).reshape(count, KVH, GQ, DH)
    cf = c_rows.astype(jnp.float32).reshape(count, KVH, GQ, DH)
    kself = kv_rows[:, :, :DH].astype(jnp.float32)
    vself = kv_rows[:, :, DH:].astype(jnp.float32)
    kf = keys_bf.astype(jnp.float32)
    vf = vals_bf.astype(jnp.float32)
    score = jnp.einsum('nkgd,ksd->nkgs', qf, kf) * scale
    own = jnp.einsum('nkgd,nkd->nkg', qf, kself) * scale
    top = jnp.maximum(lax.optimization_barrier(jnp.max(score, axis=-1)), own)
    expo = jnp.exp(score - top[..., None])
    self_exp = jnp.exp(own - top)
    total = lax.optimization_barrier(jnp.sum(expo, axis=-1)) + self_exp
    prob = expo / total[..., None]
    self_prob = self_exp / total
    weights = rounded(prob)
    self_weight = rounded(self_prob)
    out = jnp.einsum('nkgs,ksd->nkgd', weights, vf) + self_weight[..., None] * vself[:, :, None, :]
    delta = lax.optimization_barrier(jnp.sum(cf * out, axis=-1))
    dprob = jnp.einsum('nkgd,ksd->nkgs', cf, vf)
    dweights = rounded(prob * (dprob - delta[..., None]))
    grad_keys = jnp.einsum('nkgs,nkgd->ksd', dweights, qf) * scale
    grad_values = jnp.einsum('nkgs,nkgd->ksd', weights, cf)
    return (out.astype(jnp.bfloat16).reshape(count, KVH, GQ * DH), grad_keys, grad_values)

def reference(queries, cotangent, own_kv, tables, table_owner, cache_keys, cache_values, first_moment, second_moment):
    blocks = ROWS // Q_DEV
    dest = table_owner[tables[:, 0]].astype(jnp.int32)
    hit = (dest[:, None] == jnp.arange(TABLES, dtype=jnp.int32)[None, :]).astype(jnp.int32)
    hit = hit.reshape(blocks, Q_DEV, TABLES)
    before = jnp.cumsum(hit, axis=1, dtype=jnp.int32) - hit
    rank = lax.optimization_barrier(jnp.sum(before * hit, axis=2, dtype=jnp.int32))
    block_ids = jnp.arange(blocks, dtype=jnp.int32)[:, None]
    place = (dest.reshape(blocks, Q_DEV) * (blocks * CAP) + block_ids * CAP + rank).reshape(-1)

    def pack(x):
        empty = jnp.zeros((TABLES * blocks * CAP,) + x.shape[1:], x.dtype)
        return empty.at[place].set(x).reshape((TABLES, blocks * CAP) + x.shape[1:])
    keys_bf = cache_keys.astype(jnp.bfloat16)
    vals_bf = cache_values.astype(jnp.bfloat16)
    answers, grad_keys, grad_values = lax.map(one_owner, (pack(queries), pack(cotangent), pack(own_kv), keys_bf, vals_bf))
    attended = answers.reshape((TABLES * blocks * CAP,) + answers.shape[2:])[place]
    grad = jnp.stack([grad_keys, grad_values])
    new_first = 0.9 * first_moment + 0.1 * grad
    new_second = 0.95 * second_moment + 0.05 * grad * grad
    params = jnp.stack([cache_keys, cache_values])
    updated = params - 0.02 * new_first / (jnp.sqrt(new_second) + 1e-08)
    return (attended, updated[0], updated[1], new_first, new_second)
```

```python
import functools
import math

import jax
import jax.numpy as jnp
from jax import lax
from jax.experimental import pallas as pl
from jax.experimental.pallas import tpu as pltpu
from jax.sharding import PartitionSpec as P

TILE = 64
UNIT = 2
VMEM = 56 * 1024 * 1024
SPLIT = ((0, 1, 2), (3,))


def nt(a, b):
    return lax.dot_general(a, b, (((1,), (1,)), ((), ())), preferred_element_type=jnp.float32)


def tn(a, b):
    return lax.dot_general(a, b, (((0,), (0,)), ((), ())), preferred_element_type=jnp.float32)


def nn(a, b):
    return jnp.dot(a, b, preferred_element_type=jnp.float32)


def own_mask(rows):
    token = lax.broadcasted_iota(jnp.int32, (TILE, rows), 0)
    row = lax.broadcasted_iota(jnp.int32, (TILE, rows), 1)
    return token == row % TILE


def pick_own(mask, product):
    return jnp.sum(jnp.where(mask, product, 0.0), axis=0, keepdims=True)


def sort_kernel(slot_ref, qm, qo, cm, co, km, ko, q_out, c_out, kv_out):
    places = kv_out.shape[1]
    n = qm.shape[1]
    index = lax.broadcasted_iota(jnp.int32, (places, n), 0)
    one_m = (index == slot_ref[:, :n]).astype(jnp.bfloat16)
    one_o = (index == slot_ref[:, n:]).astype(jnp.bfloat16)

    def moved(mine, other):
        return (nn(one_m, mine[0]) + nn(one_o, other[0])).astype(jnp.bfloat16)

    head_dim = q_out.shape[3]
    for mine, other, out in ((qm, qo, q_out), (cm, co, c_out)):
        rows = moved(mine, other)
        for i in range(out.shape[1]):
            for g in range(out.shape[2] // TILE):
                out[0, i, g * TILE : (g + 1) * TILE, :] = rows[
                    i * TILE : (i + 1) * TILE, g * head_dim : (g + 1) * head_dim
                ]
    kv_out[0] = moved(km, ko)


def sort_tokens(slot, tiles, q, c, kv):
    heads, n, width = q[0].shape
    head_dim = kv[0].shape[2] // 2
    groups = width // head_dim

    def spec(x):
        return pl.BlockSpec((1,) + x.shape[1:], lambda h: (h, 0, 0))

    rows = jax.ShapeDtypeStruct((heads, tiles, groups * TILE, head_dim), jnp.bfloat16)
    row_spec = pl.BlockSpec((1,) + rows.shape[1:], lambda h: (h, 0, 0, 0))
    flops = 2 * heads * tiles * TILE * 2 * n * (2 * width + 2 * head_dim)
    return pl.pallas_call(
        sort_kernel,
        grid=(heads,),
        in_specs=[pl.BlockSpec(slot.shape, lambda h: (0, 0))]
        + [spec(x) for x in (*q, *c, *kv)],
        out_specs=[
            row_spec,
            row_spec,
            pl.BlockSpec((1, tiles * TILE, 2 * head_dim), lambda h: (h, 0, 0)),
        ],
        out_shape=[
            rows,
            rows,
            jax.ShapeDtypeStruct((heads, tiles * TILE, 2 * head_dim), jnp.bfloat16),
        ],
        compiler_params=pltpu.CompilerParams(vmem_limit_bytes=VMEM),
        cost_estimate=pl.CostEstimate(flops=flops, bytes_accessed=2 << 23, transcendentals=0),
        name="sort_tokens",
    )(slot, *q, *c, *kv)


def keys_kernel(js, meta, q_ref, c_ref, kv_ref, *refs):
    k_refs, (stat_ref, *dv_refs) = refs[: len(js)], refs[len(js) :]
    head_dim = q_ref.shape[3]
    rows = q_ref.shape[2]
    n_j = meta.shape[0] // 2
    factor = head_dim ** (-0.5) * math.log2(math.e)
    mask = own_mask(rows)
    for j, k_ref, dv_ref in zip(js, k_refs, dv_refs):
        dv_ref[...] = jnp.zeros_like(dv_ref)

        @pl.loop(meta[j], meta[j] + meta[n_j + j])
        def _(i):
            q = q_ref[0, i]
            at = pl.multiple_of(i * TILE, TILE)
            own = pick_own(mask, nt(kv_ref[0, pl.ds(at, TILE), :head_dim], q)) * factor
            score = nt(k_ref[0], q) * factor
            top = jnp.maximum(jnp.max(score, axis=0, keepdims=True), own)
            e = jnp.exp2(score - top)
            own_e = jnp.exp2(own - top)
            inverse = 1.0 / (jnp.sum(e, axis=0, keepdims=True) + own_e)
            weights = (e * inverse).astype(jnp.bfloat16)
            stat_ref[0, i, 0:1, :] = top
            stat_ref[0, i, 1:2, :] = inverse
            stat_ref[0, i, 2:3, :] = own_e * inverse
            dv_ref[0] += nn(weights, c_ref[0, i])


def values_kernel(js, meta, q_ref, c_ref, kv_ref, stat_ref, *refs):
    k_refs, v_refs = refs[: len(js)], refs[len(js) : 2 * len(js)]
    out_ref, *dk_refs = refs[2 * len(js) :]
    head_dim = q_ref.shape[3]
    rows = q_ref.shape[2]
    n_j = meta.shape[0] // 2
    scale = head_dim ** (-0.5)
    factor = scale * math.log2(math.e)
    mask = own_mask(rows)
    out_ref[...] = jnp.zeros_like(out_ref)
    for j, k_ref, v_ref, dk_ref in zip(js, k_refs, v_refs, dk_refs):
        dk_ref[...] = jnp.zeros_like(dk_ref)

        @pl.loop(meta[j], meta[j] + meta[n_j + j])
        def _(i):
            q, c = q_ref[0, i], c_ref[0, i]
            at = pl.multiple_of(i * TILE, TILE)
            own_value = kv_ref[0, pl.ds(at, TILE), head_dim:]
            own_w = stat_ref[0, i, 2:3, :].astype(jnp.bfloat16).astype(jnp.float32)
            prob = (
                jnp.exp2(nt(k_ref[0], q) * factor - stat_ref[0, i, 0:1, :])
                * stat_ref[0, i, 1:2, :]
            )
            weights = prob.astype(jnp.bfloat16)
            dprob = nt(v_ref[0], c)
            delta = jnp.sum(
                weights.astype(jnp.float32) * dprob, axis=0, keepdims=True
            ) + own_w * pick_own(mask, nt(own_value, c))
            dk_ref[0] += nn((prob * (dprob - delta)).astype(jnp.bfloat16), q) * scale
            own_part = jnp.where(mask, jnp.broadcast_to(own_w, mask.shape), 0.0)
            out = tn(v_ref[0], weights) + tn(own_value, own_part.astype(jnp.bfloat16))
            out = out.T.astype(jnp.bfloat16)
            for g in range(rows // TILE):
                out_ref[0, pl.ds(at, TILE), g * head_dim : (g + 1) * head_dim] = out[
                    g * TILE : (g + 1) * TILE
                ]


def attend(kernel, js, first_head, meta, q, c, kv, stat, tables):
    tiles, rows, head_dim = q.shape[1:]
    slots = tables[0].shape[1]
    phase_values = stat is not None

    def head_spec(x, offset):
        zeros = (0,) * (x.ndim - 1)
        return pl.BlockSpec((1,) + x.shape[1:], lambda h, m: (h + offset,) + zeros)

    grads = [jax.ShapeDtypeStruct((UNIT, slots, head_dim), jnp.float32) for j in js]
    if phase_values:
        lead = jax.ShapeDtypeStruct((UNIT, tiles * TILE, rows // TILE * head_dim), jnp.bfloat16)
    else:
        lead = jax.ShapeDtypeStruct((UNIT, tiles, 8, rows), jnp.float32)
    operands = [q, c, kv]
    in_specs = [head_spec(x, first_head) for x in operands]
    rest = ([stat] if phase_values else []) + list(tables)
    in_specs += [head_spec(x, 0) for x in rest]
    outs = [lead] + grads
    share = len(js) * UNIT * 2 * rows * slots
    return pl.pallas_call(
        functools.partial(kernel, js),
        grid_spec=pltpu.PrefetchScalarGridSpec(
            num_scalar_prefetch=1,
            grid=(UNIT,),
            in_specs=in_specs,
            out_specs=[head_spec(x, 0) for x in outs],
        ),
        out_shape=outs,
        compiler_params=pltpu.CompilerParams(vmem_limit_bytes=VMEM),
        cost_estimate=pl.CostEstimate(
            flops=(10 if phase_values else 4) * share * head_dim,
            bytes_accessed=4 << 20,
            transcendentals=share,
        ),
        name="values_phase" if phase_values else "keys_phase",
    )(meta, *operands, *rest)


def unsort_kernel(parts, slot_ref, *refs):
    sources, (mine, other) = refs[:parts], refs[parts:]
    n = mine.shape[1]
    places = sources[0].shape[1]
    index = lax.broadcasted_iota(jnp.int32, (n, places), 1)
    rows = sources[0][0]
    for source in sources[1:]:
        rows = rows + source[0]
    for half, out in enumerate((mine, other)):
        one = (index == slot_ref[half * n : (half + 1) * n, :]).astype(jnp.bfloat16)
        out[0] = nn(one, rows).astype(jnp.bfloat16)


def unsort(slot_column, sources):
    heads, places, width = sources[0].shape
    n = slot_column.shape[0] // 2
    out = jax.ShapeDtypeStruct((heads, n, width), jnp.bfloat16)
    out_spec = pl.BlockSpec((1, n, width), lambda h: (h, 0, 0))
    return pl.pallas_call(
        functools.partial(unsort_kernel, len(sources)),
        grid=(heads,),
        in_specs=[pl.BlockSpec(slot_column.shape, lambda h: (0, 0))]
        + [pl.BlockSpec((1, places, width), lambda h: (h, 0, 0)) for x in sources],
        out_specs=[out_spec, out_spec],
        out_shape=[out, out],
        compiler_params=pltpu.CompilerParams(vmem_limit_bytes=VMEM),
        cost_estimate=pl.CostEstimate(
            flops=4 * heads * n * places * width, bytes_accessed=2 << 20, transcendentals=0
        ),
        name="unsort_answers",
    )(slot_column, *sources)


def swap(x):
    return lax.ppermute(x, "rep", [(0, 1), (1, 0)])


def outward(n, step):
    right = [(2 * z, 2 * z + 2) for z in range(step - 1, n - 1)]
    left = [(2 * z + 1, 2 * z - 1) for z in range(1, n - step + 1)]
    return right + left


def homeward(n, distance):
    left = [(2 * z, 2 * z - 2) for z in range(distance, n)]
    right = [(2 * z + 1, 2 * z + 3) for z in range(0, n - distance)]
    return left + right


def routes(tables, table_owner, n_owner, tiles):
    count = tables.shape[0]
    z, rep = lax.axis_index("owner"), lax.axis_index("rep")
    hit = tables == jnp.arange(table_owner.shape[0], dtype=jnp.int32)[None, :]
    dest = jnp.sum(jnp.where(hit, table_owner[None, :], 0), axis=1, keepdims=True, dtype=jnp.int32)
    distance = (dest - z) * (2 * rep - 1)
    at_home = ((2 * z < n_owner) == (rep == 0)).astype(jnp.int32)
    js = jnp.arange(n_owner, dtype=jnp.int32)[None, :]
    asked = (distance == js) & ((js > 0) | (at_home == 1))
    member = asked.astype(jnp.bfloat16)
    row = lax.broadcasted_iota(jnp.int32, (count, count), 0)
    column = lax.broadcasted_iota(jnp.int32, (count, count), 1)
    rank = jnp.dot(
        (column < row).astype(jnp.bfloat16), member, preferred_element_type=jnp.float32
    ).astype(jnp.int32)
    number = jnp.sum(asked.astype(jnp.int32), axis=0)
    used = (number + TILE - 1) // TILE
    start = jnp.sum(jnp.where(js < js.T, used[None, :], 0), axis=1)
    slot = jnp.sum(
        jnp.where(asked, start[None, :] * TILE + rank + 1, 0), axis=1, keepdims=True
    ) - 1
    return slot, jnp.concatenate([start, used]).astype(jnp.int32)


def move_tables(
    queries,
    cotangent,
    own_kv,
    tables,
    table_owner,
    cache_keys,
    cache_values,
    first_moment,
    second_moment,
):
    n_owner = lax.axis_size("owner")
    heads = queries.shape[1]
    half = cache_keys.shape[2]
    both = ("owner", "rep")
    tiles = 2 * queries.shape[0] // TILE + n_owner
    n_units = heads // UNIT

    travel = []
    for u in range(2 * n_units):
        cache = (cache_keys, cache_values)[u % 2]
        mine = cache[0, u // 2 * UNIT : (u // 2 + 1) * UNIT].astype(jnp.bfloat16)
        table = jnp.concatenate([mine, swap(mine)], axis=1)
        got = [table]
        for step in range(1, n_owner):
            got.append(lax.ppermute(got[-1], both, outward(n_owner, step)))
        travel.append(got)

    def by_head(x):
        mine = jnp.transpose(x, (1, 0, 2))
        return mine, swap(mine)

    slot, meta = routes(
        jnp.concatenate([tables, swap(tables)], axis=0), table_owner, n_owner, tiles
    )
    q, c, kv = sort_tokens(
        slot.reshape(1, -1), tiles, by_head(queries), by_head(cotangent), by_head(own_kv)
    )

    def homecoming(partial):
        acc = None
        for j in range(n_owner - 1, 0, -1):
            total = partial[j] if acc is None else partial[j] + acc.astype(jnp.float32)
            acc = lax.ppermute(total.astype(jnp.bfloat16), both, homeward(n_owner, j))
        total = partial[0] + acc.astype(jnp.float32)
        return total[:, :half] + swap(total[:, half:])

    calls = SPLIT if n_owner == 4 else (tuple(range(n_owner)),)
    grad_keys, grad_values, answers = [], [], []
    for p in range(n_units):
        keys, values = travel[2 * p], travel[2 * p + 1]
        stats, dv, dk, outs = {}, {}, {}, []
        for js in calls:
            stats[js], *parts = attend(
                keys_kernel, js, p * UNIT, meta, q, c, kv, None, [keys[j] for j in js]
            )
            dv.update(zip(js, parts))
        grad_values.append(homecoming(dv))
        for js in calls:
            out, *parts = attend(
                values_kernel,
                js,
                p * UNIT,
                meta,
                q,
                c,
                kv,
                stats[js],
                [keys[j] for j in js] + [values[j] for j in js],
            )
            outs.append(out)
            dk.update(zip(js, parts))
        grad_keys.append(homecoming(dk))
        mine, other = unsort(slot, outs)
        answers.append(mine + swap(other))
    attended = jnp.transpose(jnp.concatenate(answers, axis=0), (1, 0, 2))
    grad = jnp.stack([jnp.concatenate(grad_keys, 0), jnp.concatenate(grad_values, 0)])[:, None]
    new_first = 0.9 * first_moment + 0.1 * grad
    new_second = 0.95 * second_moment + 0.05 * grad * grad
    params = jnp.stack([cache_keys, cache_values])
    updated = params - 0.02 * new_first / (jnp.sqrt(new_second) + 1e-08)
    return (attended, updated[0], updated[1], new_first, new_second)


def route_tokens(
    queries,
    cotangent,
    own_kv,
    tables,
    table_owner,
    cache_keys,
    cache_values,
    first_moment,
    second_moment,
):
    n_owner = lax.axis_size("owner")
    q_dev = queries.shape[0]
    heads = queries.shape[1]
    width = queries.shape[2]
    head_dim = own_kv.shape[2] // 2
    groups = width // head_dim
    cap = 2 * q_dev // n_owner
    scale = head_dim ** (-0.5)
    table_hit = tables == jnp.arange(table_owner.shape[0], dtype=jnp.int32)[None, :]
    dest = jnp.sum(jnp.where(table_hit, table_owner[None, :], 0), axis=1, dtype=jnp.int32)
    dest_hit = (dest[:, None] == jnp.arange(n_owner, dtype=jnp.int32)[None, :]).astype(jnp.int32)
    rank = jnp.sum(
        (jnp.cumsum(dest_hit, axis=0, dtype=jnp.int32) - dest_hit) * dest_hit,
        axis=1,
        dtype=jnp.int32,
    )
    place = dest * cap + rank

    def pack(x):
        return jnp.zeros((n_owner * cap,) + x.shape[1:], x.dtype).at[place].set(x)

    sent = (
        lax.all_to_all(pack(queries), "owner", split_axis=0, concat_axis=0, tiled=True),
        lax.all_to_all(pack(cotangent), "owner", split_axis=0, concat_axis=0, tiled=True),
        lax.all_to_all(pack(own_kv), "owner", split_axis=0, concat_axis=0, tiled=True),
    )
    key_half = cache_keys[0].astype(jnp.bfloat16)
    val_half = cache_values[0].astype(jnp.bfloat16)
    q_rows, c_rows, kv_rows = sent
    key_use, val_use = (
        lax.all_gather(key_half, "rep", axis=1, tiled=True),
        lax.all_gather(val_half, "rep", axis=1, tiled=True),
    )
    count = q_rows.shape[0]
    block = 512
    n_blocks = count // block
    q_four = q_rows.reshape(count, heads, groups, head_dim)
    c_four = c_rows.reshape(count, heads, groups, head_dim)
    kself = kv_rows[:, :, :head_dim]
    vself = kv_rows[:, :, head_dim:].astype(jnp.float32)
    q_blocks = q_four.reshape(n_blocks, block, heads, groups, head_dim)
    c_blocks = c_four.reshape(n_blocks, block, heads, groups, head_dim)

    def scores_of(q_block):
        return (
            jnp.einsum("nkgd,ksd->nkgs", q_block, key_use, preferred_element_type=jnp.float32)
            * scale
        )

    def stats(q_block):
        score = scores_of(q_block)
        local_top = jnp.max(score, axis=-1)
        return (local_top, jnp.sum(jnp.exp(score - local_top[..., None]), axis=-1))

    local_top, local_total = lax.map(stats, q_blocks)
    local_top = local_top.reshape(count, heads, groups)
    local_total = local_total.reshape(count, heads, groups)
    own = jnp.einsum("nkgd,nkd->nkg", q_four, kself, preferred_element_type=jnp.float32) * scale
    top = jnp.maximum(local_top, own)
    self_exp = jnp.exp(own - top)
    total = local_total * jnp.exp(local_top - top) + self_exp
    self_weight = (self_exp / total).astype(jnp.bfloat16).astype(jnp.float32)
    top_blocks = top.reshape(n_blocks, block, heads, groups)
    total_blocks = total.reshape(n_blocks, block, heads, groups)

    def weighted(args):
        q_block, top_block, total_block = args
        prob = jnp.exp(scores_of(q_block) - top_block[..., None]) / total_block[..., None]
        return jnp.einsum(
            "nkgs,ksd->nkgd", prob.astype(jnp.bfloat16), val_use, preferred_element_type=jnp.float32
        )

    out_part = lax.map(weighted, (q_blocks, top_blocks, total_blocks)).reshape(
        count, heads, groups, head_dim
    )
    out = out_part + self_weight[..., None] * vself[:, :, None, :]
    delta = jnp.sum(c_four.astype(jnp.float32) * out, axis=-1)
    delta_blocks = delta.reshape(n_blocks, block, heads, groups)

    def backward(carry, args):
        grad_keys, grad_values = carry
        q_block, c_block, top_block, total_block, delta_block = args
        prob = jnp.exp(scores_of(q_block) - top_block[..., None]) / total_block[..., None]
        weights = prob.astype(jnp.bfloat16)
        dprob = jnp.einsum("nkgd,ksd->nkgs", c_block, val_use, preferred_element_type=jnp.float32)
        dweights = (prob * (dprob - delta_block[..., None])).astype(jnp.bfloat16)
        grad_keys = grad_keys + jnp.einsum(
            "nkgs,nkgd->ksd", dweights, q_block, preferred_element_type=jnp.float32
        )
        grad_values = grad_values + jnp.einsum(
            "nkgs,nkgd->ksd", weights, c_block, preferred_element_type=jnp.float32
        )
        return ((grad_keys, grad_values), None)

    zeros_grad = jnp.zeros(key_use.shape, jnp.float32)
    (grad_keys, grad_values), unused = lax.scan(
        backward,
        (zeros_grad, zeros_grad),
        (q_blocks, c_blocks, top_blocks, total_blocks, delta_blocks),
    )
    grad_keys = grad_keys * scale
    answer_rows = out.astype(jnp.bfloat16).reshape(count, heads, width)
    grad_keys, grad_values = (
        lax.psum_scatter(grad_keys, "rep", scatter_dimension=1, tiled=True),
        lax.psum_scatter(grad_values, "rep", scatter_dimension=1, tiled=True),
    )
    returned = lax.all_to_all(answer_rows, "owner", split_axis=0, concat_axis=0, tiled=True)
    attended = returned[place]
    grad = jnp.stack([grad_keys, grad_values])[:, None]
    new_first = 0.9 * first_moment + 0.1 * grad
    new_second = 0.95 * second_moment + 0.05 * grad * grad
    params = jnp.stack([cache_keys, cache_values])
    updated = params - 0.02 * new_first / (jnp.sqrt(new_second) + 1e-08)
    return (attended, updated[0], updated[1], new_first, new_second)


def per_device(*args):
    cap = 2 * args[0].shape[0] // lax.axis_size("owner")
    return move_tables(*args) if cap >= TILE else route_tokens(*args)


def solution(mesh):
    in_specs = (
        P(("groups", "owner", "rep"), "head", None),
        P(("groups", "owner", "rep"), "head", None),
        P(("groups", "owner", "rep"), "head", None),
        P(("groups", "owner", "rep"), None),
        P("groups"),
        P(("groups", "owner"), "head", "rep", None),
        P(("groups", "owner"), "head", "rep", None),
        P(None, ("groups", "owner"), "head", "rep", None),
        P(None, ("groups", "owner"), "head", "rep", None),
    )
    out_specs = (
        P(("groups", "owner", "rep"), "head", None),
        P(("groups", "owner"), "head", "rep", None),
        P(("groups", "owner"), "head", "rep", None),
        P(None, ("groups", "owner"), "head", "rep", None),
        P(None, ("groups", "owner"), "head", "rep", None),
    )
    return jax.shard_map(
        per_device, mesh=mesh, in_specs=in_specs, out_specs=out_specs, check_vma=False
    )
```

```python
import functools
import math

import jax
import jax.numpy as jnp
from jax import lax
from jax.experimental import pallas as pl
from jax.experimental.pallas import tpu as pltpu
from jax.sharding import PartitionSpec as P

TILE = 64
ANY = pl.BlockSpec(memory_space=pl.ANY)
HELD = pl.BlockSpec(memory_space=pltpu.VMEM)
PARAMS = pltpu.CompilerParams(vmem_limit_bytes=24 * 1024 * 1024)


def hold(x):
    return pltpu.with_memory_space_constraint(x, pltpu.VMEM)


def held(shape, dtype):
    return pltpu.VMEM(shape, dtype)


def cost(flops, size, exps=0):
    return pl.CostEstimate(flops=flops, bytes_accessed=size, transcendentals=exps)


def nt(a, b):
    return lax.dot_general(a, b, (((1,), (1,)), ((), ())), preferred_element_type=jnp.float32)


def tn(a, b):
    return lax.dot_general(a, b, (((0,), (0,)), ((), ())), preferred_element_type=jnp.float32)


def nn(a, b):
    return jnp.dot(a, b, preferred_element_type=jnp.float32)


def own_mask(rows):
    token = lax.broadcasted_iota(jnp.int32, (TILE, rows), 0)
    row = lax.broadcasted_iota(jnp.int32, (TILE, rows), 1)
    return token == row % TILE


def pick_own(mask, product):
    return jnp.sum(jnp.where(mask, product, 0.0), axis=0, keepdims=True)


def round_kernel(keys, values, out):
    out[:, 0] = keys[0].astype(out.dtype)
    out[:, 1] = values[0].astype(out.dtype)


def round_table(keys, values, first, count):
    slots, head_dim = keys.shape[2:]
    spec = pl.BlockSpec((1, 1, slots, head_dim), lambda i: (0, first + i, 0, 0))
    return pl.pallas_call(
        round_kernel,
        grid=(count,),
        in_specs=[spec, spec],
        out_specs=pl.BlockSpec((1, 2, slots, head_dim), lambda i: (i, 0, 0, 0)),
        out_shape=jax.ShapeDtypeStruct((count, 2, slots, head_dim), jnp.bfloat16),
        compiler_params=PARAMS,
        cost_estimate=cost(0, 12 * count * slots * head_dim),
        name="round_table",
    )(keys, values)


def join_kernel(mine, other, out):
    half = mine.shape[2]
    out[:, :, :half] = mine[...]
    out[:, :, half:] = other[...]


def join(mine, other):
    count, pair, slots, head_dim = mine.shape
    return pl.pallas_call(
        join_kernel,
        in_specs=[HELD, HELD],
        out_specs=HELD,
        out_shape=held((count, pair, 2 * slots, head_dim), mine.dtype),
        compiler_params=PARAMS,
        cost_estimate=cost(0, 8 * mine.size),
        name="join",
    )(hold(mine), hold(other))


def sort_kernel(slot_ref, qm, qo, cm, co, km, ko, q_out, c_out, kv_out):
    head = pl.program_id(0)
    places = kv_out.shape[1]
    n = qm.shape[1]
    index = lax.broadcasted_iota(jnp.int32, (places, n), 0)
    one_m = (index == slot_ref[0, :, :n]).astype(jnp.bfloat16)
    one_o = (index == slot_ref[0, :, n:]).astype(jnp.bfloat16)

    def moved(mine, other):
        return (nn(one_m, mine[0]) + nn(one_o, other[0])).astype(jnp.bfloat16)

    head_dim = q_out.shape[3]
    for mine, other, out in ((qm, qo, q_out), (cm, co, c_out)):
        rows = moved(mine, other)
        for i in range(out.shape[1]):
            for g in range(out.shape[2] // TILE):
                out[head, i, g * TILE : (g + 1) * TILE, :] = rows[
                    i * TILE : (i + 1) * TILE, g * head_dim : (g + 1) * head_dim
                ]
    kv_out[head] = moved(km, ko)


def sort_tokens(slot, tiles, q, c, kv):
    heads, n, width = q[0].shape
    head_dim = kv[0].shape[2] // 2
    groups = width // head_dim

    def spec(x):
        return pl.BlockSpec((1,) + x.shape[1:], lambda h: (h, 0, 0))

    rows = held((heads, tiles, groups * TILE, head_dim), jnp.bfloat16)
    flops = 2 * heads * tiles * TILE * 2 * n * (2 * width + 2 * head_dim)
    return pl.pallas_call(
        sort_kernel,
        grid=(heads,),
        in_specs=[spec(x) for x in (slot, *q, *c, *kv)],
        out_specs=[HELD, HELD, HELD],
        out_shape=[rows, rows, held((heads, tiles * TILE, 2 * head_dim), jnp.bfloat16)],
        compiler_params=PARAMS,
        cost_estimate=cost(flops, 2 << 23),
        name="sort_tokens",
    )(slot, *q, *c, *kv)


def attend_tile(q, c, own_kv, table, turned, mask):
    head_dim = q.shape[1]
    factor = head_dim ** (-0.5) * math.log2(math.e)
    own_value = own_kv[:, head_dim:]
    own = pick_own(mask, nt(own_kv[:, :head_dim], q))
    score = nt(table[0], q)
    top = jnp.maximum(jnp.max(score, axis=0, keepdims=True), own) * factor
    e = jnp.exp2(score * factor - top)
    own_e = jnp.exp2(own * factor - top)
    inverse = 1.0 / (jnp.sum(e, axis=0, keepdims=True) + own_e)
    prob = e * inverse
    weights = prob.astype(jnp.bfloat16)
    own_w = (own_e * inverse).astype(jnp.bfloat16).astype(jnp.float32)
    dprob = nt(table[1], c)
    delta = jnp.sum(weights.astype(jnp.float32) * dprob, axis=0, keepdims=True)
    delta = delta + own_w * pick_own(mask, nt(own_value, c))
    dweights = (prob * (dprob - delta)).astype(jnp.bfloat16)
    own_part = jnp.where(mask, jnp.broadcast_to(own_w, mask.shape), 0.0)
    out = nn(turned, weights) + tn(own_value, own_part.astype(jnp.bfloat16))
    return weights, dweights, out.T.astype(jnp.bfloat16)


def attend_kernel(js, far, first, n_after, meta, *refs):
    q_ref, c_ref, kv_ref, *refs = refs[n_after:]
    table_refs, (out_ref, *grad_refs) = refs[: len(js)], refs[len(js) :]
    head_dim = q_ref.shape[3]
    rows = q_ref.shape[2]
    n_j = meta.shape[0] // 2
    mask = own_mask(rows)
    out_ref[...] = jnp.zeros_like(out_ref)

    def place(i):
        return pl.ds(pl.multiple_of(i * TILE, TILE), TILE)

    for j, table, grad_ref in zip(js, table_refs, grad_refs):
        start, used = meta[j], meta[n_j + j]

        @pl.loop(0, table.shape[0])
        def _(h):
            head = first + h
            grad = grad_refs[-1] if j == far else grad_ref.at[h]
            grad[...] = jnp.zeros_like(grad)
            pair = table.at[h]
            turned = pair[1].T

            def work(indices):
                done = [
                    attend_tile(
                        q_ref[head, i], c_ref[head, i], kv_ref[head, place(i), :], pair, turned, mask
                    )
                    for i in indices
                ]
                grad[1] += sum(nn(d[0], c_ref[head, i]) for i, d in zip(indices, done))
                grad[0] += sum(nn(d[1], q_ref[head, i]) for i, d in zip(indices, done))
                for i, d in zip(indices, done):
                    for g in range(rows // TILE):
                        out_ref[h, place(i), g * head_dim : (g + 1) * head_dim] = d[2][
                            g * TILE : (g + 1) * TILE
                        ]

            @pl.loop(0, used // 2)
            def _(t):
                work([start + 2 * t, start + 2 * t + 1])

            @pl.when(used % 2 == 1)
            def _():
                work([start + used - 1])

            if j == far:
                grad_ref[h] = grad[...].astype(grad_ref.dtype)


def attend(afters, js, far, first, meta, q, c, kv, tables):
    tiles, rows, head_dim = q.shape[1:]
    count, pair, slots = tables[0].shape[:3]
    outs = [held((count, tiles * TILE, rows // TILE * head_dim), jnp.bfloat16)]
    for j in js:
        kind = jnp.bfloat16 if j == far else jnp.float32
        outs.append(held((count, pair, slots, head_dim), kind))
    share = len(js) * count * 2 * rows * slots
    operands = (q, c, kv, *tables)
    return pl.pallas_call(
        functools.partial(attend_kernel, js, far if far in js else None, first, len(afters)),
        in_specs=[pl.BlockSpec(memory_space=pltpu.SMEM)]
        + [ANY for x in afters]
        + [HELD for x in operands],
        out_specs=[HELD for x in outs],
        scratch_shapes=[pltpu.VMEM((pair, slots, head_dim), jnp.float32)] if far in js else [],
        out_shape=outs,
        compiler_params=PARAMS,
        cost_estimate=cost(10 * share * head_dim, 4 << 20, share),
        name="attend",
    )(meta, *afters, *map(hold, operands))


def hop_kernel(after, partial, acc, out):
    out[...] = (partial[...] + acc[...].astype(jnp.float32)).astype(out.dtype)


def hop(after, partial, acc):
    return pl.pallas_call(
        hop_kernel,
        in_specs=[ANY, HELD, HELD],
        out_specs=HELD,
        out_shape=held(acc.shape, acc.dtype),
        compiler_params=PARAMS,
        cost_estimate=cost(partial.size, 8 * partial.size),
        name="hop",
    )(after, hold(partial), hold(acc))


def arrive_kernel(after, partial, acc, out):
    half = out.shape[2]
    out[...] = partial[:, :, half:] + acc[:, :, half:].astype(jnp.float32)


def arrive(after, partial, acc):
    count, pair, slots, head_dim = partial.shape
    return pl.pallas_call(
        arrive_kernel,
        in_specs=[ANY, HELD, HELD],
        out_specs=HELD,
        out_shape=held((count, pair, slots // 2, head_dim), jnp.float32),
        compiler_params=PARAMS,
        cost_estimate=cost(partial.size, 5 * partial.size),
        name="arrive",
    )(after, hold(partial), hold(acc))


def adam_kernel(scale, after, partial, acc, other, keys, values, first, second, *refs):
    new_keys, new_values, new_first, new_second = refs[-4:]
    for i, (param, new) in enumerate(((keys, new_keys), (values, new_values))):
        grad = partial[0, i] + acc[0, i].astype(jnp.float32) + other[0, i]
        if i == 0:
            grad = grad * scale
        moment = 0.9 * first[i, 0, 0] + 0.1 * grad
        square = 0.95 * second[i, 0, 0] + 0.05 * grad * grad
        new_first[i, 0, 0] = moment
        new_second[i, 0, 0] = square
        new[0, 0] = param[0, 0] - 0.02 * moment / (jnp.sqrt(square) + 1e-08)


def adam(after, head, partial, acc, other, keys, values, first, second, results):
    count = partial.shape[0]
    half, head_dim = keys.shape[2:]
    blocks = 4
    rows = half // blocks
    param = pl.BlockSpec((1, 1, rows, head_dim), lambda h, i: (0, head + h, i, 0))
    moment = pl.BlockSpec((2, 1, 1, rows, head_dim), lambda h, i: (0, 0, head + h, i, 0))
    grad = pl.BlockSpec((1, 2, rows, head_dim), lambda h, i: (h, 0, i, 0))
    arrays = (keys, values, first, second)
    return pl.pallas_call(
        functools.partial(adam_kernel, head_dim ** (-0.5)),
        grid=(count, blocks),
        in_specs=[ANY, grad, grad, grad, param, param, moment, moment] + [ANY for x in results],
        out_specs=[param, param, moment, moment],
        out_shape=[jax.ShapeDtypeStruct(x.shape, x.dtype) for x in arrays],
        input_output_aliases={8 + i: i for i in range(len(results))},
        compiler_params=PARAMS,
        cost_estimate=cost(24 * half * head_dim * count, 60 * half * head_dim * count),
        name="adam",
    )(after, partial, acc, other, *arrays, *results)


def unsort_kernel(after, slot_ref, near, far, mine, other):
    n = mine.shape[1]
    index = lax.broadcasted_iota(jnp.int32, (n, near.shape[1]), 1)
    rows = near[0] + far[0]
    for half, out in enumerate((mine, other)):
        one = (index == slot_ref[0, half * n : (half + 1) * n, :]).astype(jnp.bfloat16)
        out[0] = nn(one, rows).astype(jnp.bfloat16)


def unsort(after, slot, near, far):
    heads, places, width = near.shape
    n = slot.shape[1] // 2
    out = jax.ShapeDtypeStruct((heads, n, width), jnp.bfloat16)
    out_spec = pl.BlockSpec((1, n, width), lambda h: (h, 0, 0))
    in_spec = pl.BlockSpec((1, places, width), lambda h: (h, 0, 0))
    return pl.pallas_call(
        unsort_kernel,
        grid=(heads,),
        in_specs=[ANY, pl.BlockSpec((1, 2 * n, 1), lambda h: (h, 0, 0)), in_spec, in_spec],
        out_specs=[out_spec, out_spec],
        out_shape=[out, out],
        compiler_params=PARAMS,
        cost_estimate=cost(4 * heads * n * places * width, 2 << 20),
        name="unsort_answers",
    )(after, slot, near, far)


def swap(x):
    return lax.ppermute(x, "rep", [(0, 1), (1, 0)])


def outward(n, step, flip):
    right = [(2 * z, 2 * z + 2 + flip * (z == n - 2)) for z in range(step - 1, n - 1)]
    left = [(2 * z + 1, 2 * z - 1 - flip * (z == 1)) for z in range(1, n - step + 1)]
    return right + left


def homeward(n, distance, flip):
    left = [(2 * z + flip * (z == n - 1), 2 * z - 2) for z in range(distance, n)]
    right = [(2 * z + 1 - flip * (z == 0), 2 * z + 3) for z in range(0, n - distance)]
    return left + right


def routes(tables, table_owner, n_owner, flip):
    count = tables.shape[0]
    z, rep = lax.axis_index("owner"), lax.axis_index("rep")
    if flip:
        rep = jnp.where((z == 0) | (z == n_owner - 1), 1 - rep, rep)
    hit = tables == jnp.arange(table_owner.shape[0], dtype=jnp.int32)[None, :]
    dest = jnp.sum(jnp.where(hit, table_owner[None, :], 0), axis=1, keepdims=True, dtype=jnp.int32)
    distance = (dest - z) * (2 * rep - 1)
    at_home = ((2 * z < n_owner) == (rep == 0)).astype(jnp.int32)
    js = jnp.arange(n_owner, dtype=jnp.int32)[None, :]
    asked = (distance == js) & ((js > 0) | (at_home == 1))
    member = asked.astype(jnp.bfloat16)
    row = lax.broadcasted_iota(jnp.int32, (count, count), 0)
    column = lax.broadcasted_iota(jnp.int32, (count, count), 1)
    rank = jnp.dot(
        (column < row).astype(jnp.bfloat16), member, preferred_element_type=jnp.float32
    ).astype(jnp.int32)
    number = jnp.sum(asked.astype(jnp.int32), axis=0)
    used = (number + TILE - 1) // TILE
    start = jnp.sum(jnp.where(js < js.T, used[None, :], 0), axis=1)
    slot = jnp.sum(jnp.where(asked, start[None, :] * TILE + rank + 1, 0), axis=1) - 1
    return slot, jnp.concatenate([start, used]).astype(jnp.int32)


def move_tables(
    queries,
    cotangent,
    own_kv,
    tables,
    table_owner,
    cache_keys,
    cache_values,
    first_moment,
    second_moment,
):
    n_owner = lax.axis_size("owner")
    heads = queries.shape[1]
    both = ("owner", "rep")
    tiles = 2 * queries.shape[0] // TILE + n_owner
    far = n_owner - 1

    sizes = [1] + [2] * (heads // 2 - 1) + [1]
    units = []
    for i, count in enumerate(sizes):
        first, flip = sum(sizes[:i]), i % 2
        mine = round_table(cache_keys, cache_values, first, count)
        got = [join(mine, swap(mine))]
        for step in range(1, n_owner):
            got.append(lax.ppermute(got[-1], both, outward(n_owner, step, flip)))
        units.append({"first": first, "flip": flip, "got": got})

    def by_head(x):
        mine = jnp.transpose(x, (1, 0, 2))
        return mine, swap(mine)

    asked = jnp.concatenate([tables, swap(tables)], axis=0)
    slots, metas = zip(*(routes(asked, table_owner, n_owner, flip) for flip in (0, 1)))
    slot = jnp.stack([slots[unit["flip"]] for unit, n in zip(units, sizes) for h in range(n)])
    q, c, kv = sort_tokens(
        slot[:, None, :], tiles, by_head(queries), by_head(cotangent), by_head(own_kv)
    )

    after = slot
    results = ()
    for turn in range(2 * len(units) + far + 1):
        if turn < 2 * len(units):
            u, js = turn // 2, (tuple(range(far)), (far,))[turn % 2]
            unit = units[u]
            afters = [after]
            if u + 1 < len(units):
                afters.append(units[u + 1]["got"][1 + turn % 2])
            out, *parts = attend(
                afters,
                js,
                far,
                unit["first"],
                metas[unit["flip"]],
                q,
                c,
                kv,
                [unit["got"][j] for j in js],
            )
            after = out
            unit.setdefault("outs", []).append(out)
            unit.update(zip(js, parts))
            if js == (far,):
                unit["acc"] = lax.ppermute(unit[far], both, homeward(n_owner, far, unit["flip"]))
        for u, unit in enumerate(units):
            step = turn - 2 * u - 1
            j = far - step
            if 0 < step < far:
                after = hop(after, unit[j], unit["acc"])
                unit["acc"] = lax.ppermute(after, both, homeward(n_owner, j, unit["flip"]))
            if step == far:
                after = arrive(after, unit[0], unit["acc"])
                unit["other"] = swap(after)
            if step == far + 1:
                results = adam(
                    after,
                    unit["first"],
                    unit[0],
                    unit["acc"],
                    unit["other"],
                    cache_keys,
                    cache_values,
                    first_moment,
                    second_moment,
                    results,
                )
                after = results[0]
        if turn == 2 * len(units) - 1:
            near_out, far_out = (
                jnp.concatenate([unit["outs"][i] for unit in units], axis=0) for i in range(2)
            )
            after, other = unsort(after, slot[:, :, None], near_out, far_out)
            attended = jnp.transpose(after + swap(other), (1, 0, 2))
    return (attended, *results)


def route_tokens(
    queries,
    cotangent,
    own_kv,
    tables,
    table_owner,
    cache_keys,
    cache_values,
    first_moment,
    second_moment,
):
    n_owner = lax.axis_size("owner")
    q_dev = queries.shape[0]
    heads = queries.shape[1]
    width = queries.shape[2]
    head_dim = own_kv.shape[2] // 2
    groups = width // head_dim
    cap = 2 * q_dev // n_owner
    scale = head_dim ** (-0.5)
    table_hit = tables == jnp.arange(table_owner.shape[0], dtype=jnp.int32)[None, :]
    dest = jnp.sum(jnp.where(table_hit, table_owner[None, :], 0), axis=1, dtype=jnp.int32)
    dest_hit = (dest[:, None] == jnp.arange(n_owner, dtype=jnp.int32)[None, :]).astype(jnp.int32)
    rank = jnp.sum(
        (jnp.cumsum(dest_hit, axis=0, dtype=jnp.int32) - dest_hit) * dest_hit,
        axis=1,
        dtype=jnp.int32,
    )
    place = dest * cap + rank

    def pack(x):
        return jnp.zeros((n_owner * cap,) + x.shape[1:], x.dtype).at[place].set(x)

    sent = (
        lax.all_to_all(pack(queries), "owner", split_axis=0, concat_axis=0, tiled=True),
        lax.all_to_all(pack(cotangent), "owner", split_axis=0, concat_axis=0, tiled=True),
        lax.all_to_all(pack(own_kv), "owner", split_axis=0, concat_axis=0, tiled=True),
    )
    key_half = cache_keys[0].astype(jnp.bfloat16)
    val_half = cache_values[0].astype(jnp.bfloat16)
    q_rows, c_rows, kv_rows = sent
    key_use, val_use = (
        lax.all_gather(key_half, "rep", axis=1, tiled=True),
        lax.all_gather(val_half, "rep", axis=1, tiled=True),
    )
    count = q_rows.shape[0]
    block = 512
    n_blocks = count // block
    q_four = q_rows.reshape(count, heads, groups, head_dim)
    c_four = c_rows.reshape(count, heads, groups, head_dim)
    kself = kv_rows[:, :, :head_dim]
    vself = kv_rows[:, :, head_dim:].astype(jnp.float32)
    q_blocks = q_four.reshape(n_blocks, block, heads, groups, head_dim)
    c_blocks = c_four.reshape(n_blocks, block, heads, groups, head_dim)

    def scores_of(q_block):
        return (
            jnp.einsum("nkgd,ksd->nkgs", q_block, key_use, preferred_element_type=jnp.float32)
            * scale
        )

    def stats(q_block):
        score = scores_of(q_block)
        local_top = jnp.max(score, axis=-1)
        return (local_top, jnp.sum(jnp.exp(score - local_top[..., None]), axis=-1))

    local_top, local_total = lax.map(stats, q_blocks)
    local_top = local_top.reshape(count, heads, groups)
    local_total = local_total.reshape(count, heads, groups)
    own = jnp.einsum("nkgd,nkd->nkg", q_four, kself, preferred_element_type=jnp.float32) * scale
    top = jnp.maximum(local_top, own)
    self_exp = jnp.exp(own - top)
    total = local_total * jnp.exp(local_top - top) + self_exp
    self_weight = (self_exp / total).astype(jnp.bfloat16).astype(jnp.float32)
    top_blocks = top.reshape(n_blocks, block, heads, groups)
    total_blocks = total.reshape(n_blocks, block, heads, groups)

    def weighted(args):
        q_block, top_block, total_block = args
        prob = jnp.exp(scores_of(q_block) - top_block[..., None]) / total_block[..., None]
        return jnp.einsum(
            "nkgs,ksd->nkgd", prob.astype(jnp.bfloat16), val_use, preferred_element_type=jnp.float32
        )

    out_part = lax.map(weighted, (q_blocks, top_blocks, total_blocks)).reshape(
        count, heads, groups, head_dim
    )
    out = out_part + self_weight[..., None] * vself[:, :, None, :]
    delta = jnp.sum(c_four.astype(jnp.float32) * out, axis=-1)
    delta_blocks = delta.reshape(n_blocks, block, heads, groups)

    def backward(carry, args):
        grad_keys, grad_values = carry
        q_block, c_block, top_block, total_block, delta_block = args
        prob = jnp.exp(scores_of(q_block) - top_block[..., None]) / total_block[..., None]
        weights = prob.astype(jnp.bfloat16)
        dprob = jnp.einsum("nkgd,ksd->nkgs", c_block, val_use, preferred_element_type=jnp.float32)
        dweights = (prob * (dprob - delta_block[..., None])).astype(jnp.bfloat16)
        grad_keys = grad_keys + jnp.einsum(
            "nkgs,nkgd->ksd", dweights, q_block, preferred_element_type=jnp.float32
        )
        grad_values = grad_values + jnp.einsum(
            "nkgs,nkgd->ksd", weights, c_block, preferred_element_type=jnp.float32
        )
        return ((grad_keys, grad_values), None)

    zeros_grad = jnp.zeros(key_use.shape, jnp.float32)
    (grad_keys, grad_values), unused = lax.scan(
        backward,
        (zeros_grad, zeros_grad),
        (q_blocks, c_blocks, top_blocks, total_blocks, delta_blocks),
    )
    grad_keys = grad_keys * scale
    answer_rows = out.astype(jnp.bfloat16).reshape(count, heads, width)
    grad_keys, grad_values = (
        lax.psum_scatter(grad_keys, "rep", scatter_dimension=1, tiled=True),
        lax.psum_scatter(grad_values, "rep", scatter_dimension=1, tiled=True),
    )
    returned = lax.all_to_all(answer_rows, "owner", split_axis=0, concat_axis=0, tiled=True)
    attended = returned[place]
    grad = jnp.stack([grad_keys, grad_values])[:, None]
    new_first = 0.9 * first_moment + 0.1 * grad
    new_second = 0.95 * second_moment + 0.05 * grad * grad
    params = jnp.stack([cache_keys, cache_values])
    updated = params - 0.02 * new_first / (jnp.sqrt(new_second) + 1e-08)
    return (attended, updated[0], updated[1], new_first, new_second)


def per_device(*args):
    cap = 2 * args[0].shape[0] // lax.axis_size("owner")
    return move_tables(*args) if cap >= TILE else route_tokens(*args)


def solution(mesh):
    in_specs = (
        P(("groups", "owner", "rep"), "head", None),
        P(("groups", "owner", "rep"), "head", None),
        P(("groups", "owner", "rep"), "head", None),
        P(("groups", "owner", "rep"), None),
        P("groups"),
        P(("groups", "owner"), "head", "rep", None),
        P(("groups", "owner"), "head", "rep", None),
        P(None, ("groups", "owner"), "head", "rep", None),
        P(None, ("groups", "owner"), "head", "rep", None),
    )
    out_specs = (
        P(("groups", "owner", "rep"), "head", None),
        P(("groups", "owner"), "head", "rep", None),
        P(("groups", "owner"), "head", "rep", None),
        P(None, ("groups", "owner"), "head", "rep", None),
        P(None, ("groups", "owner"), "head", "rep", None),
    )
    return jax.shard_map(
        per_device, mesh=mesh, in_specs=in_specs, out_specs=out_specs, check_vma=False
    )
```

```python
import functools
import math

import jax
import jax.numpy as jnp
from jax import lax
from jax.experimental import pallas as pl
from jax.experimental.pallas import tpu as pltpu
from jax.sharding import PartitionSpec as P

SORTED = 4
TILE = 64
ANY = pl.BlockSpec(memory_space=pl.ANY)
HELD = pl.BlockSpec(memory_space=pltpu.VMEM)
PARAMS = pltpu.CompilerParams(vmem_limit_bytes=24 * 1024 * 1024)


def hold(x):
    return pltpu.with_memory_space_constraint(x, pltpu.VMEM)


def held(shape, dtype):
    return pltpu.VMEM(shape, dtype)


QUICK = pl.CostEstimate(flops=1, bytes_accessed=1, transcendentals=0)
SLOW = pl.CostEstimate(flops=10**11, bytes_accessed=1, transcendentals=0)


def nt(a, b):
    return lax.dot_general(a, b, (((1,), (1,)), ((), ())), preferred_element_type=jnp.float32)


def tn(a, b):
    return lax.dot_general(a, b, (((0,), (0,)), ((), ())), preferred_element_type=jnp.float32)


def nn(a, b):
    return jnp.dot(a, b, preferred_element_type=jnp.float32)


def own_mask(rows):
    token = lax.broadcasted_iota(jnp.int32, (TILE, rows), 0)
    row = lax.broadcasted_iota(jnp.int32, (TILE, rows), 1)
    return token == row % TILE


def pick_own(mask, product):
    return jnp.sum(jnp.where(mask, product, 0.0), axis=0, keepdims=True)


def round_kernel(keys, values, out):
    out[:, 0] = keys[0].astype(out.dtype)
    out[:, 1] = values[0].astype(out.dtype)


def round_table(keys, values, first, count):
    slots, head_dim = keys.shape[2:]
    spec = pl.BlockSpec((1, 1, slots, head_dim), lambda i: (0, first + i, 0, 0))
    return pl.pallas_call(
        round_kernel,
        grid=(count,),
        in_specs=[spec, spec],
        out_specs=pl.BlockSpec((1, 2, slots, head_dim), lambda i: (i, 0, 0, 0)),
        out_shape=jax.ShapeDtypeStruct((count, 2, slots, head_dim), jnp.bfloat16),
        compiler_params=PARAMS,
        cost_estimate=QUICK,
        name="round_table",
    )(keys, values)


def join_kernel(mine, other, *outs):
    half = mine.shape[2]
    for i, out in enumerate(outs):
        out[0, :, :half] = mine[i]
        out[0, :, half:] = other[i]


def join(mine, other):
    heads, pair, slots, head_dim = mine.shape
    return pl.pallas_call(
        join_kernel,
        in_specs=[HELD, HELD],
        out_specs=[HELD] * heads,
        out_shape=[held((1, pair, 2 * slots, head_dim), mine.dtype)] * heads,
        compiler_params=PARAMS,
        cost_estimate=SLOW,
        name="join",
    )(hold(mine), hold(other))


def tie_kernel(x, after, out):
    pass


def tie(x, after):
    return pl.pallas_call(
        tie_kernel,
        in_specs=[HELD, ANY],
        out_specs=HELD,
        out_shape=held(x.shape, x.dtype),
        input_output_aliases={0: 0},
        compiler_params=PARAMS,
        cost_estimate=QUICK,
        name="tie",
    )(hold(x), after)


def sort_kernel(after, meta_a, meta_b, slot_ref, qm, qo, cm, co, km, ko, q_out, c_out, kv_out):
    head = pl.program_id(0)
    n = qm.shape[1]
    head_dim = q_out.shape[3]
    last = meta_a.shape[0] // 2 - 1
    used = jnp.where(
        head % 2 == 0,
        meta_a[last] + meta_a[2 * last + 1],
        meta_b[last] + meta_b[2 * last + 1],
    )
    rows = SORTED * TILE

    for part in range(q_out.shape[1] // SORTED):

        @pl.when(part * SORTED < used)
        def _():
            index = lax.broadcasted_iota(jnp.int32, (rows, n), 0) + part * rows
            one_m = (index == slot_ref[head, :, :n]).astype(jnp.bfloat16)
            one_o = (index == slot_ref[head, :, n:]).astype(jnp.bfloat16)

            def moved(mine, other):
                return (nn(one_m, mine[head]) + nn(one_o, other[head])).astype(jnp.bfloat16)

            for mine, other, out in ((qm, qo, q_out), (cm, co, c_out)):
                x = moved(mine, other)
                for i in range(SORTED):
                    for g in range(out.shape[2] // TILE):
                        out[head, part * SORTED + i, g * TILE : (g + 1) * TILE, :] = x[
                            i * TILE : (i + 1) * TILE, g * head_dim : (g + 1) * head_dim
                        ]
            kv_out[head, part * rows : (part + 1) * rows, :] = moved(km, ko)


def sort_tokens(after, metas, slot, tiles, q, c, kv):
    heads, n, width = q[0].shape
    head_dim = kv[0].shape[2] // 2
    groups = width // head_dim
    operands = (slot, *q, *c, *kv)
    rows = held((heads, tiles, groups * TILE, head_dim), jnp.bfloat16)
    return pl.pallas_call(
        sort_kernel,
        grid=(heads,),
        in_specs=[ANY]
        + [pl.BlockSpec(memory_space=pltpu.SMEM) for x in metas]
        + [HELD for x in operands],
        out_specs=[HELD, HELD, HELD],
        out_shape=[rows, rows, held((heads, tiles * TILE, 2 * head_dim), jnp.bfloat16)],
        compiler_params=PARAMS,
        cost_estimate=QUICK,
        name="sort_tokens",
    )(after, *metas, *map(hold, operands))


def attend_tile(q, c, own_kv, table, turned, mask):
    head_dim = q.shape[1]
    factor = head_dim ** (-0.5) * math.log2(math.e)
    own_value = own_kv[:, head_dim:]
    own = pick_own(mask, nt(own_kv[:, :head_dim], q))
    score = nt(table[0], q)
    top = jnp.maximum(jnp.max(score, axis=0, keepdims=True), own) * factor
    e = jnp.exp2(score * factor - top)
    own_e = jnp.exp2(own * factor - top)
    inverse = 1.0 / (jnp.sum(e, axis=0, keepdims=True) + own_e)
    prob = e * inverse
    weights = prob.astype(jnp.bfloat16)
    own_w = (own_e * inverse).astype(jnp.bfloat16).astype(jnp.float32)
    dprob = nt(table[1], c)
    delta = jnp.sum(weights.astype(jnp.float32) * dprob, axis=0, keepdims=True)
    delta = delta + own_w * pick_own(mask, nt(own_value, c))
    dweights = (prob * (dprob - delta)).astype(jnp.bfloat16)
    own_part = jnp.where(mask, jnp.broadcast_to(own_w, mask.shape), 0.0)
    out = nn(turned, weights) + tn(own_value, own_part.astype(jnp.bfloat16))
    return weights, dweights, out.T.astype(jnp.bfloat16)


def attend_kernel(js, far, first, n_after, meta, *refs):
    q_ref, c_ref, kv_ref, *refs = refs[n_after:]
    table_refs, (out_ref, *grad_refs) = refs[: len(js)], refs[len(js) :]
    head_dim = q_ref.shape[3]
    rows = q_ref.shape[2]
    n_j = meta.shape[0] // 2
    mask = own_mask(rows)
    out_ref[...] = jnp.zeros_like(out_ref)

    def place(i):
        return pl.ds(pl.multiple_of(i * TILE, TILE), TILE)

    for j, table, grad_ref in zip(js, table_refs, grad_refs):
        start, used = meta[j], meta[n_j + j]

        @pl.loop(0, table.shape[0])
        def _(h):
            head = first + h
            grad = grad_refs[-1] if j == far else grad_ref.at[h]
            grad[...] = jnp.zeros_like(grad)
            pair = table.at[h]
            turned = pair[1].T

            def work(indices):
                done = [
                    attend_tile(
                        q_ref[head, i], c_ref[head, i], kv_ref[head, place(i), :], pair, turned, mask
                    )
                    for i in indices
                ]
                grad[1] += sum(nn(d[0], c_ref[head, i]) for i, d in zip(indices, done))
                grad[0] += sum(nn(d[1], q_ref[head, i]) for i, d in zip(indices, done))
                for i, d in zip(indices, done):
                    for g in range(rows // TILE):
                        out_ref[h, place(i), g * head_dim : (g + 1) * head_dim] = d[2][
                            g * TILE : (g + 1) * TILE
                        ]

            @pl.loop(0, used // 2)
            def _(t):
                work([start + 2 * t, start + 2 * t + 1])

            @pl.when(used % 2 == 1)
            def _():
                work([start + used - 1])

            if j == far:
                grad_ref[h] = grad[...].astype(grad_ref.dtype)


def attend(afters, js, far, first, meta, q, c, kv, tables):
    tiles, rows, head_dim = q.shape[1:]
    count, pair, slots = tables[0].shape[:3]
    outs = [held((count, tiles * TILE, rows // TILE * head_dim), jnp.bfloat16)]
    for j in js:
        kind = jnp.bfloat16 if j == far else jnp.float32
        outs.append(held((count, pair, slots, head_dim), kind))
    operands = (q, c, kv, *tables)
    return pl.pallas_call(
        functools.partial(attend_kernel, js, far if far in js else None, first, len(afters)),
        in_specs=[pl.BlockSpec(memory_space=pltpu.SMEM)]
        + [ANY for x in afters]
        + [HELD for x in operands],
        out_specs=[HELD for x in outs],
        scratch_shapes=[pltpu.VMEM((pair, slots, head_dim), jnp.float32)] if far in js else [],
        out_shape=outs,
        compiler_params=PARAMS,
        cost_estimate=QUICK,
        name="attend",
    )(meta, *afters, *map(hold, operands))


def hop_kernel(*refs):
    partial, acc, out = refs[-3:]
    out[...] = (partial[...] + acc[...].astype(jnp.float32)).astype(out.dtype)


def hop(afters, partial, acc):
    return pl.pallas_call(
        hop_kernel,
        in_specs=[ANY for x in afters] + [HELD, HELD],
        out_specs=HELD,
        out_shape=held(acc.shape, acc.dtype),
        compiler_params=PARAMS,
        cost_estimate=QUICK,
        name="hop",
    )(*afters, hold(partial), hold(acc))


def arrive_kernel(*refs):
    partial, acc, out = refs[-3:]
    half = out.shape[2]
    out[...] = partial[:, :, half:] + acc[:, :, half:].astype(jnp.float32)


def arrive(afters, partial, acc):
    count, pair, slots, head_dim = partial.shape
    return pl.pallas_call(
        arrive_kernel,
        in_specs=[ANY for x in afters] + [HELD, HELD],
        out_specs=HELD,
        out_shape=held((count, pair, slots // 2, head_dim), jnp.float32),
        compiler_params=PARAMS,
        cost_estimate=QUICK,
        name="arrive",
    )(*afters, hold(partial), hold(acc))


def adam_kernel(scale, *refs):
    partial, acc, other, keys, values, first, second = refs[:7]
    new_keys, new_values, new_first, new_second = refs[-4:]
    rows = keys.shape[2]
    at = pl.ds(pl.multiple_of(pl.program_id(0) * rows, rows), rows)
    for i, (param, new) in enumerate(((keys, new_keys), (values, new_values))):
        grad = partial[0, i, at, :] + acc[0, i, at, :].astype(jnp.float32) + other[0, i, at, :]
        if i == 0:
            grad = grad * scale
        moment = 0.9 * first[i, 0, 0] + 0.1 * grad
        square = 0.95 * second[i, 0, 0] + 0.05 * grad * grad
        new_first[i, 0, 0] = moment
        new_second[i, 0, 0] = square
        new[0, 0] = param[0, 0] - 0.02 * moment / (jnp.sqrt(square) + 1e-08)


def adam(head, partial, acc, other, keys, values, first, second, results):
    half, head_dim = keys.shape[2:]
    blocks = 2
    rows = half // blocks
    param = pl.BlockSpec((1, 1, rows, head_dim), lambda i: (0, head, i, 0))
    moment = pl.BlockSpec((2, 1, 1, rows, head_dim), lambda i: (0, 0, head, i, 0))
    arrays = (keys, values, first, second)
    return pl.pallas_call(
        functools.partial(adam_kernel, head_dim ** (-0.5)),
        grid=(blocks,),
        in_specs=[HELD, HELD, HELD, param, param, moment, moment] + [ANY for x in results],
        out_specs=[param, param, moment, moment],
        out_shape=[jax.ShapeDtypeStruct(x.shape, x.dtype) for x in arrays],
        input_output_aliases={7 + i: i for i in range(len(results))},
        compiler_params=PARAMS,
        cost_estimate=QUICK,
        name="adam",
    )(hold(partial), hold(acc), hold(other), *arrays, *results)


def unsort_kernel(slot_ref, *refs):
    sources, (mine, other) = refs[:-2], refs[-2:]
    heads, n = mine.shape[:2]
    index = lax.broadcasted_iota(jnp.int32, (n, sources[0].shape[1]), 1)
    for h in range(heads):
        rows = sources[2 * h][0] + sources[2 * h + 1][0]
        slot = jnp.broadcast_to(slot_ref[h].astype(jnp.float32), (8, 2 * n)).T[:, :1]
        for half, out in enumerate((mine, other)):
            one = (index == slot[half * n : (half + 1) * n].astype(jnp.int32)).astype(jnp.bfloat16)
            out[h] = nn(one, rows).astype(jnp.bfloat16)


def unsort(slot, sources):
    heads, n = slot.shape[0], slot.shape[2] // 2
    out = held((heads, n, sources[0].shape[2]), jnp.bfloat16)
    return pl.pallas_call(
        unsort_kernel,
        in_specs=[HELD] + [HELD for x in sources],
        out_specs=[HELD, HELD],
        out_shape=[out, out],
        compiler_params=PARAMS,
        cost_estimate=QUICK,
        name="unsort_answers",
    )(hold(slot), *map(hold, sources))


def swap(x):
    return lax.ppermute(x, "rep", [(0, 1), (1, 0)])


def end_core(side, distance, unit):
    return side ^ ((unit + distance + 1) & 1)


def outward(n, step, unit):
    right = [(2 * z, 2 * z + 2) for z in range(step - 1, n - 2)]
    right.append((2 * n - 4, 2 * n - 2 + end_core(0, step, unit)))
    left = [(2 * z + 1, 2 * z - 1) for z in range(2, n - step + 1)]
    left.append((3, end_core(1, step, unit)))
    return right + left


def homeward(n, distance, unit):
    left = [(2 * z, 2 * z - 2) for z in range(distance, n - 1)]
    left.append((2 * n - 2 + end_core(0, distance, unit), 2 * n - 4))
    right = [(2 * z + 1, 2 * z + 3) for z in range(1, n - distance)]
    right.append((end_core(1, distance, unit), 3))
    return left + right


def routes(tables, table_owner, n_owner, unit):
    count = tables.shape[0]
    z, rep = lax.axis_index("owner"), lax.axis_index("rep")
    hit = tables == jnp.arange(table_owner.shape[0], dtype=jnp.int32)[None, :]
    dest = jnp.sum(jnp.where(hit, table_owner[None, :], 0), axis=1, keepdims=True, dtype=jnp.int32)
    js = jnp.arange(n_owner, dtype=jnp.int32)[None, :]
    home = (2 * z >= n_owner).astype(jnp.int32)
    core = jnp.where(dest == z, home, (dest > z).astype(jnp.int32))
    away = jnp.abs(dest - z)
    at_end = (z == 0) | (z == n_owner - 1)
    core = jnp.where(at_end, end_core((z == 0).astype(jnp.int32), away, unit), core)
    asked = (away == js) & (core == rep)
    member = asked.astype(jnp.bfloat16)
    row = lax.broadcasted_iota(jnp.int32, (count, count), 0)
    column = lax.broadcasted_iota(jnp.int32, (count, count), 1)
    rank = jnp.dot(
        (column < row).astype(jnp.bfloat16), member, preferred_element_type=jnp.float32
    ).astype(jnp.int32)
    number = jnp.sum(asked.astype(jnp.int32), axis=0)
    used = (number + TILE - 1) // TILE
    start = jnp.sum(jnp.where(js < js.T, used[None, :], 0), axis=1)
    slot = jnp.sum(jnp.where(asked, start[None, :] * TILE + rank + 1, 0), axis=1) - 1
    return slot, jnp.concatenate([start, used]).astype(jnp.int32)


def move_tables(
    queries,
    cotangent,
    own_kv,
    tables,
    table_owner,
    cache_keys,
    cache_values,
    first_moment,
    second_moment,
):
    n_owner = lax.axis_size("owner")
    heads = queries.shape[1]
    both = ("owner", "rep")
    tiles = -(-(2 * queries.shape[0] // TILE + n_owner - 1) // SORTED) * SORTED
    far = n_owner - 1

    mine = round_table(cache_keys, cache_values, 0, heads)
    mine, queries, cotangent, own_kv = lax.optimization_barrier(
        (mine, queries, cotangent, own_kv)
    )
    units = [{"got": [table]} for table in join(mine, swap(mine))]

    def send(turn, after):
        for u, unit in enumerate(units):
            step = turn - u + 1
            if 1 <= step < n_owner:
                if turn > 1:
                    unit["got"][-1] = tie(unit["got"][-1], after)
                unit["got"].append(
                    lax.ppermute(unit["got"][-1], both, outward(n_owner, step, u % 2))
                )

    def by_head(x):
        mine = jnp.transpose(x, (1, 0, 2))
        return mine, swap(mine)

    asked = jnp.concatenate([tables, swap(tables)], axis=0)
    slots, metas = zip(*(routes(asked, table_owner, n_owner, flip) for flip in (0, 1)))
    slot = jnp.stack([slots[u % 2] for u in range(heads)])[:, None, :]
    send(0, None)
    send(1, None)
    q, c, kv = sort_tokens(
        units[0]["got"][1], metas, slot, tiles, by_head(queries), by_head(cotangent), by_head(own_kv)
    )

    for turn in range(2, far):
        send(turn, kv)

    order = []
    for u in range(heads):
        order.append((2 * u, u, "near", 0))
        order.append((min(2 * u + 3, 2 * heads), u, "far", 0))
        order += [(2 * u + 2 * k + 3.1, u, "hop", far - k) for k in range(1, far)]
        order.append((2 * u + 2 * far + 3.2, u, "arrive", 0))

    after = kv
    results = ()
    for _, u, what, j in sorted(order):
        unit = units[u]
        if what in ("near", "far"):
            js = tuple(range(far)) if what == "near" else (far,)
            out, *parts = attend(
                [after], js, far, u, metas[u % 2], q, c, kv, [unit["got"][j] for j in js]
            )
            after = out
            unit[what] = out
            unit.update(zip(js, parts))
            if what == "near":
                send(u + far, after)
            if what == "far":
                unit["acc"] = lax.ppermute(unit[far], both, homeward(n_owner, far, u % 2))
                if u == heads - 1:
                    mine, other = unsort(
                        slot, [x[what] for x in units for what in ("near", "far")]
                    )
                    attended = jnp.transpose(mine + swap(other), (1, 0, 2))
        if what == "hop":
            after = hop([after], unit[j], unit["acc"])
            unit["acc"] = lax.ppermute(after, both, homeward(n_owner, j, u % 2))
        if what == "arrive":
            last = [attended, results[0]] if u == heads - 1 else []
            after = arrive([after] + last, unit[0], unit["acc"])
            results = adam(
                u,
                unit[0],
                unit["acc"],
                swap(after),
                cache_keys,
                cache_values,
                first_moment,
                second_moment,
                results,
            )
    return (attended, *results)


def route_tokens(
    queries,
    cotangent,
    own_kv,
    tables,
    table_owner,
    cache_keys,
    cache_values,
    first_moment,
    second_moment,
):
    n_owner = lax.axis_size("owner")
    q_dev = queries.shape[0]
    heads = queries.shape[1]
    width = queries.shape[2]
    head_dim = own_kv.shape[2] // 2
    groups = width // head_dim
    cap = 2 * q_dev // n_owner
    scale = head_dim ** (-0.5)
    table_hit = tables == jnp.arange(table_owner.shape[0], dtype=jnp.int32)[None, :]
    dest = jnp.sum(jnp.where(table_hit, table_owner[None, :], 0), axis=1, dtype=jnp.int32)
    dest_hit = (dest[:, None] == jnp.arange(n_owner, dtype=jnp.int32)[None, :]).astype(jnp.int32)
    rank = jnp.sum(
        (jnp.cumsum(dest_hit, axis=0, dtype=jnp.int32) - dest_hit) * dest_hit,
        axis=1,
        dtype=jnp.int32,
    )
    place = dest * cap + rank

    def pack(x):
        return jnp.zeros((n_owner * cap,) + x.shape[1:], x.dtype).at[place].set(x)

    sent = (
        lax.all_to_all(pack(queries), "owner", split_axis=0, concat_axis=0, tiled=True),
        lax.all_to_all(pack(cotangent), "owner", split_axis=0, concat_axis=0, tiled=True),
        lax.all_to_all(pack(own_kv), "owner", split_axis=0, concat_axis=0, tiled=True),
    )
    key_half = cache_keys[0].astype(jnp.bfloat16)
    val_half = cache_values[0].astype(jnp.bfloat16)
    q_rows, c_rows, kv_rows = sent
    key_use, val_use = (
        lax.all_gather(key_half, "rep", axis=1, tiled=True),
        lax.all_gather(val_half, "rep", axis=1, tiled=True),
    )
    count = q_rows.shape[0]
    block = 512
    n_blocks = count // block
    q_four = q_rows.reshape(count, heads, groups, head_dim)
    c_four = c_rows.reshape(count, heads, groups, head_dim)
    kself = kv_rows[:, :, :head_dim]
    vself = kv_rows[:, :, head_dim:].astype(jnp.float32)
    q_blocks = q_four.reshape(n_blocks, block, heads, groups, head_dim)
    c_blocks = c_four.reshape(n_blocks, block, heads, groups, head_dim)

    def scores_of(q_block):
        return (
            jnp.einsum("nkgd,ksd->nkgs", q_block, key_use, preferred_element_type=jnp.float32)
            * scale
        )

    def stats(q_block):
        score = scores_of(q_block)
        local_top = jnp.max(score, axis=-1)
        return (local_top, jnp.sum(jnp.exp(score - local_top[..., None]), axis=-1))

    local_top, local_total = lax.map(stats, q_blocks)
    local_top = local_top.reshape(count, heads, groups)
    local_total = local_total.reshape(count, heads, groups)
    own = jnp.einsum("nkgd,nkd->nkg", q_four, kself, preferred_element_type=jnp.float32) * scale
    top = jnp.maximum(local_top, own)
    self_exp = jnp.exp(own - top)
    total = local_total * jnp.exp(local_top - top) + self_exp
    self_weight = (self_exp / total).astype(jnp.bfloat16).astype(jnp.float32)
    top_blocks = top.reshape(n_blocks, block, heads, groups)
    total_blocks = total.reshape(n_blocks, block, heads, groups)

    def weighted(args):
        q_block, top_block, total_block = args
        prob = jnp.exp(scores_of(q_block) - top_block[..., None]) / total_block[..., None]
        return jnp.einsum(
            "nkgs,ksd->nkgd", prob.astype(jnp.bfloat16), val_use, preferred_element_type=jnp.float32
        )

    out_part = lax.map(weighted, (q_blocks, top_blocks, total_blocks)).reshape(
        count, heads, groups, head_dim
    )
    out = out_part + self_weight[..., None] * vself[:, :, None, :]
    delta = jnp.sum(c_four.astype(jnp.float32) * out, axis=-1)
    delta_blocks = delta.reshape(n_blocks, block, heads, groups)

    def backward(carry, args):
        grad_keys, grad_values = carry
        q_block, c_block, top_block, total_block, delta_block = args
        prob = jnp.exp(scores_of(q_block) - top_block[..., None]) / total_block[..., None]
        weights = prob.astype(jnp.bfloat16)
        dprob = jnp.einsum("nkgd,ksd->nkgs", c_block, val_use, preferred_element_type=jnp.float32)
        dweights = (prob * (dprob - delta_block[..., None])).astype(jnp.bfloat16)
        grad_keys = grad_keys + jnp.einsum(
            "nkgs,nkgd->ksd", dweights, q_block, preferred_element_type=jnp.float32
        )
        grad_values = grad_values + jnp.einsum(
            "nkgs,nkgd->ksd", weights, c_block, preferred_element_type=jnp.float32
        )
        return ((grad_keys, grad_values), None)

    zeros_grad = jnp.zeros(key_use.shape, jnp.float32)
    (grad_keys, grad_values), unused = lax.scan(
        backward,
        (zeros_grad, zeros_grad),
        (q_blocks, c_blocks, top_blocks, total_blocks, delta_blocks),
    )
    grad_keys = grad_keys * scale
    answer_rows = out.astype(jnp.bfloat16).reshape(count, heads, width)
    grad_keys, grad_values = (
        lax.psum_scatter(grad_keys, "rep", scatter_dimension=1, tiled=True),
        lax.psum_scatter(grad_values, "rep", scatter_dimension=1, tiled=True),
    )
    returned = lax.all_to_all(answer_rows, "owner", split_axis=0, concat_axis=0, tiled=True)
    attended = returned[place]
    grad = jnp.stack([grad_keys, grad_values])[:, None]
    new_first = 0.9 * first_moment + 0.1 * grad
    new_second = 0.95 * second_moment + 0.05 * grad * grad
    params = jnp.stack([cache_keys, cache_values])
    updated = params - 0.02 * new_first / (jnp.sqrt(new_second) + 1e-08)
    return (attended, updated[0], updated[1], new_first, new_second)


def per_device(*args):
    cap = 2 * args[0].shape[0] // lax.axis_size("owner")
    return move_tables(*args) if cap >= TILE else route_tokens(*args)


def solution(mesh):
    in_specs = (
        P(("groups", "owner", "rep"), "head", None),
        P(("groups", "owner", "rep"), "head", None),
        P(("groups", "owner", "rep"), "head", None),
        P(("groups", "owner", "rep"), None),
        P("groups"),
        P(("groups", "owner"), "head", "rep", None),
        P(("groups", "owner"), "head", "rep", None),
        P(None, ("groups", "owner"), "head", "rep", None),
        P(None, ("groups", "owner"), "head", "rep", None),
    )
    out_specs = (
        P(("groups", "owner", "rep"), "head", None),
        P(("groups", "owner"), "head", "rep", None),
        P(("groups", "owner"), "head", "rep", None),
        P(None, ("groups", "owner"), "head", "rep", None),
        P(None, ("groups", "owner"), "head", "rep", None),
    )
    return jax.shard_map(
        per_device, mesh=mesh, in_specs=in_specs, out_specs=out_specs, check_vma=False
    )
```

```python
import functools
import math

import jax
import jax.numpy as jnp
from jax import lax
from jax.experimental import pallas as pl
from jax.experimental.pallas import tpu as pltpu
from jax.sharding import PartitionSpec as P

SORTED = 4
TILE = 64
ANY = pl.BlockSpec(memory_space=pl.ANY)
HELD = pl.BlockSpec(memory_space=pltpu.VMEM)
PARAMS = pltpu.CompilerParams(vmem_limit_bytes=12 * 1024 * 1024)


def hold(x):
    return pltpu.with_memory_space_constraint(x, pltpu.VMEM)


def outside(x):
    return pltpu.with_memory_space_constraint(x, pltpu.HBM)


def held(shape, dtype):
    return pltpu.VMEM(shape, dtype)


QUICK = pl.CostEstimate(flops=1, bytes_accessed=1, transcendentals=0)
SLOW = pl.CostEstimate(flops=10**11, bytes_accessed=1, transcendentals=0)


def nt(a, b):
    return lax.dot_general(a, b, (((1,), (1,)), ((), ())), preferred_element_type=jnp.float32)


def tn(a, b):
    return lax.dot_general(a, b, (((0,), (0,)), ((), ())), preferred_element_type=jnp.float32)


def nn(a, b):
    return jnp.dot(a, b, preferred_element_type=jnp.float32)


def own_mask(rows):
    token = lax.broadcasted_iota(jnp.int32, (TILE, rows), 0)
    row = lax.broadcasted_iota(jnp.int32, (TILE, rows), 1)
    return token == row % TILE


def pick_own(mask, product):
    return jnp.sum(jnp.where(mask, product, 0.0), axis=0, keepdims=True)


def round_kernel(keys, values, out):
    count = keys.shape[1]
    at = pl.ds(pl.program_id(0) * count, count)
    out[at, 0] = keys[0].astype(out.dtype)
    out[at, 1] = values[0].astype(out.dtype)


def round_table(keys, values):
    heads, slots, head_dim = keys.shape[1:]
    spec = pl.BlockSpec((1, heads // 2, slots, head_dim), lambda i: (0, i, 0, 0))
    return pl.pallas_call(
        round_kernel,
        grid=(2,),
        in_specs=[spec, spec],
        out_specs=HELD,
        out_shape=held((heads, 2, slots, head_dim), jnp.bfloat16),
        compiler_params=PARAMS,
        cost_estimate=QUICK,
        name="round_table",
    )(outside(keys), outside(values))


def join_kernel(mine, other, *outs):
    half = mine.shape[2]
    for i, out in enumerate(outs):
        out[0, :, :half] = mine[i]
        out[0, :, half:] = other[i]


def join(mine, other):
    heads, pair, slots, head_dim = mine.shape
    return pl.pallas_call(
        join_kernel,
        in_specs=[HELD, HELD],
        out_specs=[HELD] * heads,
        out_shape=[held((1, pair, 2 * slots, head_dim), mine.dtype)] * heads,
        compiler_params=PARAMS,
        cost_estimate=SLOW,
        name="join",
    )(hold(mine), hold(other))


def tie_kernel(x, after, out):
    out[...] = x[...]


def tie(x, after):
    return pl.pallas_call(
        tie_kernel,
        in_specs=[HELD, ANY],
        out_specs=HELD,
        out_shape=held(x.shape, x.dtype),
        input_output_aliases={0: 0},
        compiler_params=PARAMS,
        cost_estimate=QUICK,
        name="tie",
    )(hold(x), after)


def sort_kernel(after, meta_a, meta_b, slot_ref, qm, qo, cm, co, km, ko, q_out, c_out, kv_out):
    head = pl.program_id(0)
    n = qm.shape[1]
    head_dim = q_out.shape[3]
    last = meta_a.shape[0] // 2 - 1
    used = jnp.where(
        head % 2 == 0,
        meta_a[last] + meta_a[2 * last + 1],
        meta_b[last] + meta_b[2 * last + 1],
    )
    rows = SORTED * TILE

    for part in range(q_out.shape[1] // SORTED):

        @pl.when(part * SORTED < used)
        def _():
            index = lax.broadcasted_iota(jnp.int32, (rows, n), 0) + part * rows
            one_m = (index == slot_ref[head, :, :n]).astype(jnp.bfloat16)
            one_o = (index == slot_ref[head, :, n:]).astype(jnp.bfloat16)

            def moved(mine, other):
                return (nn(one_m, mine[head]) + nn(one_o, other[head])).astype(jnp.bfloat16)

            for mine, other, out in ((qm, qo, q_out), (cm, co, c_out)):
                x = moved(mine, other)
                for i in range(SORTED):
                    for g in range(out.shape[2] // TILE):
                        out[head, part * SORTED + i, g * TILE : (g + 1) * TILE, :] = x[
                            i * TILE : (i + 1) * TILE, g * head_dim : (g + 1) * head_dim
                        ]
            kv_out[head, part * rows : (part + 1) * rows, :] = moved(km, ko)


def sort_tokens(after, metas, slot, tiles, q, c, kv):
    heads, n, width = q[0].shape
    head_dim = kv[0].shape[2] // 2
    groups = width // head_dim
    operands = (slot, *q, *c, *kv)
    rows = held((heads, tiles, groups * TILE, head_dim), jnp.bfloat16)
    return pl.pallas_call(
        sort_kernel,
        grid=(heads,),
        in_specs=[ANY]
        + [pl.BlockSpec(memory_space=pltpu.SMEM) for x in metas]
        + [HELD for x in operands],
        out_specs=[HELD, HELD, HELD],
        out_shape=[rows, rows, held((heads, tiles * TILE, 2 * head_dim), jnp.bfloat16)],
        compiler_params=PARAMS,
        cost_estimate=QUICK,
        name="sort_tokens",
    )(after, *metas, *map(hold, operands))


def attend_tile(q, c, own_kv, table, turned, mask):
    head_dim = q.shape[1]
    factor = head_dim ** (-0.5) * math.log2(math.e)
    own_value = own_kv[:, head_dim:]
    own = pick_own(mask, nt(own_kv[:, :head_dim], q))
    score = nt(table[0], q)
    top = jnp.maximum(jnp.max(score, axis=0, keepdims=True), own) * factor
    e = jnp.exp2(score * factor - top)
    own_e = jnp.exp2(own * factor - top)
    inverse = 1.0 / (jnp.sum(e, axis=0, keepdims=True) + own_e)
    prob = e * inverse
    weights = prob.astype(jnp.bfloat16)
    own_w = (own_e * inverse).astype(jnp.bfloat16).astype(jnp.float32)
    dprob = nt(table[1], c)
    delta = jnp.sum(weights.astype(jnp.float32) * dprob, axis=0, keepdims=True)
    delta = delta + own_w * pick_own(mask, nt(own_value, c))
    dweights = (prob * (dprob - delta)).astype(jnp.bfloat16)
    own_part = jnp.where(mask, jnp.broadcast_to(own_w, mask.shape), 0.0)
    out = nn(turned, weights) + tn(own_value, own_part.astype(jnp.bfloat16))
    return weights, dweights, out.T.astype(jnp.bfloat16)


def attend_kernel(js, far, first, n_after, meta, *refs):
    q_ref, c_ref, kv_ref, *refs = refs[n_after:]
    table_refs, (out_ref, *grad_refs) = refs[: len(js)], refs[len(js) :]
    head_dim = q_ref.shape[3]
    rows = q_ref.shape[2]
    n_j = meta.shape[0] // 2
    mask = own_mask(rows)
    out_ref[...] = jnp.zeros_like(out_ref)

    def place(i):
        return pl.ds(pl.multiple_of(i * TILE, TILE), TILE)

    for j, table, grad_ref in zip(js, table_refs, grad_refs):
        start, used = meta[j], meta[n_j + j]

        @pl.loop(0, table.shape[0])
        def _(h):
            head = first + h
            grad = grad_refs[-1] if j == far else grad_ref.at[h]
            grad[...] = jnp.zeros_like(grad)
            pair = table.at[h]
            turned = pair[1].T

            def work(indices):
                done = [
                    attend_tile(
                        q_ref[head, i], c_ref[head, i], kv_ref[head, place(i), :], pair, turned, mask
                    )
                    for i in indices
                ]
                grad[1] += sum(nn(d[0], c_ref[head, i]) for i, d in zip(indices, done))
                grad[0] += sum(nn(d[1], q_ref[head, i]) for i, d in zip(indices, done))
                for i, d in zip(indices, done):
                    for g in range(rows // TILE):
                        out_ref[h, place(i), g * head_dim : (g + 1) * head_dim] = d[2][
                            g * TILE : (g + 1) * TILE
                        ]

            @pl.loop(0, used // 2)
            def _(t):
                work([start + 2 * t, start + 2 * t + 1])

            @pl.when(used % 2 == 1)
            def _():
                work([start + used - 1])

            if j == far:
                grad_ref[h] = grad[...].astype(grad_ref.dtype)


def attend(afters, js, far, first, meta, q, c, kv, tables):
    tiles, rows, head_dim = q.shape[1:]
    count, pair, slots = tables[0].shape[:3]
    outs = [held((count, tiles * TILE, rows // TILE * head_dim), jnp.bfloat16)]
    for j in js:
        kind = jnp.bfloat16 if j == far else jnp.float32
        outs.append(held((count, pair, slots, head_dim), kind))
    operands = (q, c, kv, *tables)
    return pl.pallas_call(
        functools.partial(attend_kernel, js, far if far in js else None, first, len(afters)),
        in_specs=[pl.BlockSpec(memory_space=pltpu.SMEM)]
        + [ANY for x in afters]
        + [HELD for x in operands],
        out_specs=[HELD for x in outs],
        scratch_shapes=[pltpu.VMEM((pair, slots, head_dim), jnp.float32)] if far in js else [],
        out_shape=outs,
        compiler_params=PARAMS,
        cost_estimate=QUICK,
        name="attend",
    )(meta, *afters, *map(hold, operands))


def hop_kernel(*refs):
    partial, acc, out = refs[-3:]
    out[...] = (partial[...] + acc[...].astype(jnp.float32)).astype(out.dtype)


def hop(afters, partial, acc):
    return pl.pallas_call(
        hop_kernel,
        in_specs=[ANY for x in afters] + [HELD, HELD],
        out_specs=HELD,
        out_shape=held(acc.shape, acc.dtype),
        compiler_params=PARAMS,
        cost_estimate=QUICK,
        name="hop",
    )(*afters, hold(partial), hold(acc))


def arrive_kernel(*refs):
    partial, acc, out = refs[-3:]
    half = out.shape[2]
    out[...] = partial[:, :, half:] + acc[:, :, half:].astype(jnp.float32)


def arrive(afters, partial, acc):
    count, pair, slots, head_dim = partial.shape
    return pl.pallas_call(
        arrive_kernel,
        in_specs=[ANY for x in afters] + [HELD, HELD],
        out_specs=HELD,
        out_shape=held((count, pair, slots // 2, head_dim), jnp.float32),
        compiler_params=PARAMS,
        cost_estimate=QUICK,
        name="arrive",
    )(*afters, hold(partial), hold(acc))


def adam_kernel(scale, *refs):
    partial, acc, other, keys, values, first, second = refs[:7]
    new_keys, new_values, new_first, new_second = refs[-4:]
    rows = keys.shape[2]
    at = pl.ds(pl.multiple_of(pl.program_id(0) * rows, rows), rows)
    for i, (param, new) in enumerate(((keys, new_keys), (values, new_values))):
        grad = partial[0, i, at, :] + acc[0, i, at, :].astype(jnp.float32) + other[0, i, at, :]
        if i == 0:
            grad = grad * scale
        moment = 0.9 * first[i, 0, 0] + 0.1 * grad
        square = 0.95 * second[i, 0, 0] + 0.05 * grad * grad
        new_first[i, 0, 0] = moment
        new_second[i, 0, 0] = square
        new[0, 0] = param[0, 0] - 0.02 * moment / (jnp.sqrt(square) + 1e-08)


def adam(head, partial, acc, other, keys, values, first, second, results):
    half, head_dim = keys.shape[2:]
    blocks = 2
    rows = half // blocks
    param = pl.BlockSpec((1, 1, rows, head_dim), lambda i: (0, head, i, 0))
    moment = pl.BlockSpec((2, 1, 1, rows, head_dim), lambda i: (0, 0, head, i, 0))
    arrays = (keys, values, first, second)
    return pl.pallas_call(
        functools.partial(adam_kernel, head_dim ** (-0.5)),
        grid=(blocks,),
        in_specs=[HELD, HELD, HELD, param, param, moment, moment] + [ANY for x in results],
        out_specs=[param, param, moment, moment],
        out_shape=[jax.ShapeDtypeStruct(x.shape, x.dtype) for x in arrays],
        input_output_aliases={7 + i: i for i in range(len(results))},
        compiler_params=PARAMS,
        cost_estimate=QUICK,
        name="adam",
    )(hold(partial), hold(acc), hold(other), *arrays, *results)


def unsort_kernel(after, slot_ref, *refs):
    sources, (mine, other) = refs[:-2], refs[-2:]
    heads, n = mine.shape[:2]
    index = lax.broadcasted_iota(jnp.int32, (n, sources[0].shape[1]), 1)
    for h in range(heads):
        rows = sources[2 * h][0] + sources[2 * h + 1][0]
        slot = jnp.broadcast_to(slot_ref[h].astype(jnp.float32), (8, 2 * n)).T[:, :1]
        for half, out in enumerate((mine, other)):
            one = (index == slot[half * n : (half + 1) * n].astype(jnp.int32)).astype(jnp.bfloat16)
            out[h] = nn(one, rows).astype(jnp.bfloat16)


def unsort(after, slot, sources):
    heads, n = slot.shape[0], slot.shape[2] // 2
    out = held((heads, n, sources[0].shape[2]), jnp.bfloat16)
    return pl.pallas_call(
        unsort_kernel,
        in_specs=[ANY, HELD] + [HELD for x in sources],
        out_specs=[HELD, HELD],
        out_shape=[out, out],
        compiler_params=PARAMS,
        cost_estimate=QUICK,
        name="unsort_answers",
    )(after, hold(slot), *map(hold, sources))


def swap(x):
    return lax.ppermute(x, "rep", [(0, 1), (1, 0)])


def end_core(side, distance, unit):
    return side ^ ((unit + distance + 1) & 1)


def outward(n, step, unit):
    right = [(2 * z, 2 * z + 2) for z in range(step - 1, n - 2)]
    right.append((2 * n - 4, 2 * n - 2 + end_core(0, step, unit)))
    left = [(2 * z + 1, 2 * z - 1) for z in range(2, n - step + 1)]
    left.append((3, end_core(1, step, unit)))
    return right + left


def homeward(n, distance, unit):
    left = [(2 * z, 2 * z - 2) for z in range(distance, n - 1)]
    left.append((2 * n - 2 + end_core(0, distance, unit), 2 * n - 4))
    right = [(2 * z + 1, 2 * z + 3) for z in range(1, n - distance)]
    right.append((end_core(1, distance, unit), 3))
    return left + right


def routes(tables, table_owner, n_owner, unit):
    count = tables.shape[0]
    z, rep = lax.axis_index("owner"), lax.axis_index("rep")
    hit = tables == jnp.arange(table_owner.shape[0], dtype=jnp.int32)[None, :]
    dest = jnp.sum(jnp.where(hit, table_owner[None, :], 0), axis=1, keepdims=True, dtype=jnp.int32)
    js = jnp.arange(n_owner, dtype=jnp.int32)[None, :]
    home = (2 * z >= n_owner).astype(jnp.int32)
    core = jnp.where(dest == z, home, (dest > z).astype(jnp.int32))
    away = jnp.abs(dest - z)
    at_end = (z == 0) | (z == n_owner - 1)
    core = jnp.where(at_end, end_core((z == 0).astype(jnp.int32), away, unit), core)
    asked = (away == js) & (core == rep)
    member = asked.astype(jnp.bfloat16)
    row = lax.broadcasted_iota(jnp.int32, (count, count), 0)
    column = lax.broadcasted_iota(jnp.int32, (count, count), 1)
    rank = jnp.dot(
        (column < row).astype(jnp.bfloat16), member, preferred_element_type=jnp.float32
    ).astype(jnp.int32)
    number = jnp.sum(asked.astype(jnp.int32), axis=0)
    used = (number + TILE - 1) // TILE
    start = jnp.sum(jnp.where(js < js.T, used[None, :], 0), axis=1)
    slot = jnp.sum(jnp.where(asked, start[None, :] * TILE + rank + 1, 0), axis=1) - 1
    return slot, jnp.concatenate([start, used]).astype(jnp.int32)


def move_tables(
    queries,
    cotangent,
    own_kv,
    tables,
    table_owner,
    cache_keys,
    cache_values,
    first_moment,
    second_moment,
):
    n_owner = lax.axis_size("owner")
    heads = queries.shape[1]
    both = ("owner", "rep")
    tiles = -(-(2 * queries.shape[0] // TILE + n_owner - 1) // SORTED) * SORTED
    far = n_owner - 1

    mine = round_table(cache_keys, cache_values)
    mine, queries, cotangent, own_kv = lax.optimization_barrier(
        (mine, queries, cotangent, own_kv)
    )
    units = [{"got": [table]} for table in join(mine, swap(mine))]

    def send(turn, after):
        for u, unit in enumerate(units):
            step = turn - u + 1
            if 1 <= step < n_owner:
                if turn > 1:
                    unit["got"][-1] = tie(unit["got"][-1], after)
                unit["got"].append(
                    lax.ppermute(unit["got"][-1], both, outward(n_owner, step, u % 2))
                )

    def by_head(x):
        mine = jnp.transpose(x, (1, 0, 2))
        return mine, swap(mine)

    asked = jnp.concatenate([tables, swap(tables)], axis=0)
    slots, metas = zip(*(routes(asked, table_owner, n_owner, unit) for unit in (0, 1)))
    slot = jnp.stack([slots[u % 2] for u in range(heads)])[:, None, :]
    send(0, None)
    send(1, None)
    q, c, kv = sort_tokens(
        units[0]["got"][1], metas, slot, tiles, by_head(queries), by_head(cotangent), by_head(own_kv)
    )

    for turn in range(2, far):
        send(turn, kv)

    order = []
    for u in range(heads):
        order.append((2 * u, u, "near", 0))
        order.append((min(2 * u + 3, 2 * heads), u, "far", 0))
        order.append((2 * u + 5.1, u, "hop", far - 1))
        order += [(2 * u + 6.1 + 2 * (k - 2), u, "hop", far - k) for k in range(2, far)]
        order.append((2 * u + 9.2, u, "arrive", 0))

    after = kv
    results = before = ()
    for _, u, what, j in sorted(order):
        unit = units[u]
        if what in ("near", "far"):
            js = tuple(range(far)) if what == "near" else (far,)
            out, *parts = attend(
                [after], js, far, u, metas[u % 2], q, c, kv, [unit["got"][j] for j in js]
            )
            after = out
            unit[what] = out
            unit.update(zip(js, parts))
            if what == "near":
                send(u + far, after)
            if what == "far":
                unit["acc"] = lax.ppermute(unit[far], both, homeward(n_owner, far, u % 2))
        if what == "hop":
            after = hop([after], unit[j], unit["acc"])
            unit["acc"] = lax.ppermute(after, both, homeward(n_owner, j, u % 2))
            if u == heads - 1 and j == far - 1:
                mine, other = unsort(
                    after, slot, [x[what] for x in units for what in ("near", "far")]
                )
                attended = jnp.transpose(mine + swap(other), (1, 0, 2))
        if what == "arrive":
            last = [outside(attended), outside(before[0])] if u == heads - 1 else []
            after = arrive([after] + last, unit[0], unit["acc"])
            before = results
            results = adam(
                u,
                unit[0],
                unit["acc"],
                swap(after),
                cache_keys,
                cache_values,
                first_moment,
                second_moment,
                results,
            )
    return (attended, *results)


def route_tokens(
    queries,
    cotangent,
    own_kv,
    tables,
    table_owner,
    cache_keys,
    cache_values,
    first_moment,
    second_moment,
):
    n_owner = lax.axis_size("owner")
    q_dev = queries.shape[0]
    heads = queries.shape[1]
    width = queries.shape[2]
    head_dim = own_kv.shape[2] // 2
    groups = width // head_dim
    cap = 2 * q_dev // n_owner
    scale = head_dim ** (-0.5)
    table_hit = tables == jnp.arange(table_owner.shape[0], dtype=jnp.int32)[None, :]
    dest = jnp.sum(jnp.where(table_hit, table_owner[None, :], 0), axis=1, dtype=jnp.int32)
    dest_hit = (dest[:, None] == jnp.arange(n_owner, dtype=jnp.int32)[None, :]).astype(jnp.int32)
    rank = jnp.sum(
        (jnp.cumsum(dest_hit, axis=0, dtype=jnp.int32) - dest_hit) * dest_hit,
        axis=1,
        dtype=jnp.int32,
    )
    place = dest * cap + rank

    def pack(x):
        return jnp.zeros((n_owner * cap,) + x.shape[1:], x.dtype).at[place].set(x)

    sent = (
        lax.all_to_all(pack(queries), "owner", split_axis=0, concat_axis=0, tiled=True),
        lax.all_to_all(pack(cotangent), "owner", split_axis=0, concat_axis=0, tiled=True),
        lax.all_to_all(pack(own_kv), "owner", split_axis=0, concat_axis=0, tiled=True),
    )
    key_half = cache_keys[0].astype(jnp.bfloat16)
    val_half = cache_values[0].astype(jnp.bfloat16)
    q_rows, c_rows, kv_rows = sent
    key_use, val_use = (
        lax.all_gather(key_half, "rep", axis=1, tiled=True),
        lax.all_gather(val_half, "rep", axis=1, tiled=True),
    )
    count = q_rows.shape[0]
    block = 512
    n_blocks = count // block
    q_four = q_rows.reshape(count, heads, groups, head_dim)
    c_four = c_rows.reshape(count, heads, groups, head_dim)
    kself = kv_rows[:, :, :head_dim]
    vself = kv_rows[:, :, head_dim:].astype(jnp.float32)
    q_blocks = q_four.reshape(n_blocks, block, heads, groups, head_dim)
    c_blocks = c_four.reshape(n_blocks, block, heads, groups, head_dim)

    def scores_of(q_block):
        return (
            jnp.einsum("nkgd,ksd->nkgs", q_block, key_use, preferred_element_type=jnp.float32)
            * scale
        )

    def stats(q_block):
        score = scores_of(q_block)
        local_top = jnp.max(score, axis=-1)
        return (local_top, jnp.sum(jnp.exp(score - local_top[..., None]), axis=-1))

    local_top, local_total = lax.map(stats, q_blocks)
    local_top = local_top.reshape(count, heads, groups)
    local_total = local_total.reshape(count, heads, groups)
    own = jnp.einsum("nkgd,nkd->nkg", q_four, kself, preferred_element_type=jnp.float32) * scale
    top = jnp.maximum(local_top, own)
    self_exp = jnp.exp(own - top)
    total = local_total * jnp.exp(local_top - top) + self_exp
    self_weight = (self_exp / total).astype(jnp.bfloat16).astype(jnp.float32)
    top_blocks = top.reshape(n_blocks, block, heads, groups)
    total_blocks = total.reshape(n_blocks, block, heads, groups)

    def weighted(args):
        q_block, top_block, total_block = args
        prob = jnp.exp(scores_of(q_block) - top_block[..., None]) / total_block[..., None]
        return jnp.einsum(
            "nkgs,ksd->nkgd", prob.astype(jnp.bfloat16), val_use, preferred_element_type=jnp.float32
        )

    out_part = lax.map(weighted, (q_blocks, top_blocks, total_blocks)).reshape(
        count, heads, groups, head_dim
    )
    out = out_part + self_weight[..., None] * vself[:, :, None, :]
    delta = jnp.sum(c_four.astype(jnp.float32) * out, axis=-1)
    delta_blocks = delta.reshape(n_blocks, block, heads, groups)

    def backward(carry, args):
        grad_keys, grad_values = carry
        q_block, c_block, top_block, total_block, delta_block = args
        prob = jnp.exp(scores_of(q_block) - top_block[..., None]) / total_block[..., None]
        weights = prob.astype(jnp.bfloat16)
        dprob = jnp.einsum("nkgd,ksd->nkgs", c_block, val_use, preferred_element_type=jnp.float32)
        dweights = (prob * (dprob - delta_block[..., None])).astype(jnp.bfloat16)
        grad_keys = grad_keys + jnp.einsum(
            "nkgs,nkgd->ksd", dweights, q_block, preferred_element_type=jnp.float32
        )
        grad_values = grad_values + jnp.einsum(
            "nkgs,nkgd->ksd", weights, c_block, preferred_element_type=jnp.float32
        )
        return ((grad_keys, grad_values), None)

    zeros_grad = jnp.zeros(key_use.shape, jnp.float32)
    (grad_keys, grad_values), unused = lax.scan(
        backward,
        (zeros_grad, zeros_grad),
        (q_blocks, c_blocks, top_blocks, total_blocks, delta_blocks),
    )
    grad_keys = grad_keys * scale
    answer_rows = out.astype(jnp.bfloat16).reshape(count, heads, width)
    grad_keys, grad_values = (
        lax.psum_scatter(grad_keys, "rep", scatter_dimension=1, tiled=True),
        lax.psum_scatter(grad_values, "rep", scatter_dimension=1, tiled=True),
    )
    returned = lax.all_to_all(answer_rows, "owner", split_axis=0, concat_axis=0, tiled=True)
    attended = returned[place]
    grad = jnp.stack([grad_keys, grad_values])[:, None]
    new_first = 0.9 * first_moment + 0.1 * grad
    new_second = 0.95 * second_moment + 0.05 * grad * grad
    params = jnp.stack([cache_keys, cache_values])
    updated = params - 0.02 * new_first / (jnp.sqrt(new_second) + 1e-08)
    return (attended, updated[0], updated[1], new_first, new_second)


def per_device(*args):
    cap = 2 * args[0].shape[0] // lax.axis_size("owner")
    return move_tables(*args) if cap >= TILE else route_tokens(*args)


def solution(mesh):
    in_specs = (
        P(("groups", "owner", "rep"), "head", None),
        P(("groups", "owner", "rep"), "head", None),
        P(("groups", "owner", "rep"), "head", None),
        P(("groups", "owner", "rep"), None),
        P("groups"),
        P(("groups", "owner"), "head", "rep", None),
        P(("groups", "owner"), "head", "rep", None),
        P(None, ("groups", "owner"), "head", "rep", None),
        P(None, ("groups", "owner"), "head", "rep", None),
    )
    out_specs = (
        P(("groups", "owner", "rep"), "head", None),
        P(("groups", "owner"), "head", "rep", None),
        P(("groups", "owner"), "head", "rep", None),
        P(None, ("groups", "owner"), "head", "rep", None),
        P(None, ("groups", "owner"), "head", "rep", None),
    )
    return jax.shard_map(
        per_device, mesh=mesh, in_specs=in_specs, out_specs=out_specs, check_vma=False
    )
```

```python
import functools
import math

import jax
import jax.numpy as jnp
from jax import lax
from jax.experimental import pallas as pl
from jax.experimental.pallas import tpu as pltpu
from jax.sharding import PartitionSpec as P

SORTED = 4
TILE = 64
ANY = pl.BlockSpec(memory_space=pl.ANY)
HELD = pl.BlockSpec(memory_space=pltpu.VMEM)
PARAMS = pltpu.CompilerParams(vmem_limit_bytes=12 * 1024 * 1024)


def hold(x):
    return pltpu.with_memory_space_constraint(x, pltpu.VMEM)


def outside(x):
    return pltpu.with_memory_space_constraint(x, pltpu.HBM)


def held(shape, dtype):
    return pltpu.VMEM(shape, dtype)


QUICK = pl.CostEstimate(flops=1, bytes_accessed=1, transcendentals=0)
SLOW = pl.CostEstimate(flops=10**11, bytes_accessed=1, transcendentals=0)


def nt(a, b):
    return lax.dot_general(a, b, (((1,), (1,)), ((), ())), preferred_element_type=jnp.float32)


def tn(a, b):
    return lax.dot_general(a, b, (((0,), (0,)), ((), ())), preferred_element_type=jnp.float32)


def nn(a, b):
    return jnp.dot(a, b, preferred_element_type=jnp.float32)


def own_mask(rows):
    token = lax.broadcasted_iota(jnp.int32, (TILE, rows), 0)
    row = lax.broadcasted_iota(jnp.int32, (TILE, rows), 1)
    return token == row % TILE


def pick_own(mask, product):
    return jnp.sum(jnp.where(mask, product, 0.0), axis=0, keepdims=True)


def round_kernel(keys, values, out):
    count = keys.shape[1]
    at = pl.ds(pl.program_id(0) * count, count)
    out[at, 0] = keys[0].astype(out.dtype)
    out[at, 1] = values[0].astype(out.dtype)


def round_table(keys, values):
    heads, slots, head_dim = keys.shape[1:]
    spec = pl.BlockSpec((1, heads // 2, slots, head_dim), lambda i: (0, i, 0, 0))
    return pl.pallas_call(
        round_kernel,
        grid=(2,),
        in_specs=[spec, spec],
        out_specs=HELD,
        out_shape=held((heads, 2, slots, head_dim), jnp.bfloat16),
        compiler_params=PARAMS,
        cost_estimate=QUICK,
        name="round_table",
    )(outside(keys), outside(values))


def join_kernel(mine, other, *outs):
    half = mine.shape[2]
    for i, out in enumerate(outs):
        out[0, :, :half] = mine[i]
        out[0, :, half:] = other[i]


def join(mine, other):
    heads, pair, slots, head_dim = mine.shape
    return pl.pallas_call(
        join_kernel,
        in_specs=[HELD, HELD],
        out_specs=[HELD] * heads,
        out_shape=[held((1, pair, 2 * slots, head_dim), mine.dtype)] * heads,
        compiler_params=PARAMS,
        cost_estimate=SLOW,
        name="join",
    )(hold(mine), hold(other))


def tie_kernel(x, after, out):
    out[...] = x[...]


def tie(x, after):
    return pl.pallas_call(
        tie_kernel,
        in_specs=[HELD, ANY],
        out_specs=HELD,
        out_shape=held(x.shape, x.dtype),
        input_output_aliases={0: 0},
        compiler_params=PARAMS,
        cost_estimate=QUICK,
        name="tie",
    )(hold(x), after)


def sort_kernel(after, meta_a, meta_b, slot_ref, qm, qo, cm, co, km, ko, q_out, c_out, kv_out):
    head = pl.program_id(0)
    n = qm.shape[1]
    head_dim = q_out.shape[3]
    last = meta_a.shape[0] // 2 - 1
    used = jnp.where(
        head % 2 == 0,
        meta_a[last] + meta_a[2 * last + 1],
        meta_b[last] + meta_b[2 * last + 1],
    )
    rows = SORTED * TILE

    for part in range(q_out.shape[1] // SORTED):

        @pl.when(part * SORTED < used)
        def _():
            index = lax.broadcasted_iota(jnp.int32, (rows, n), 0) + part * rows
            one_m = (index == slot_ref[head, :, :n]).astype(jnp.bfloat16)
            one_o = (index == slot_ref[head, :, n:]).astype(jnp.bfloat16)

            def moved(mine, other):
                return (nn(one_m, mine[head]) + nn(one_o, other[head])).astype(jnp.bfloat16)

            for mine, other, out in ((qm, qo, q_out), (cm, co, c_out)):
                x = moved(mine, other)
                for i in range(SORTED):
                    for g in range(out.shape[2] // TILE):
                        out[head, part * SORTED + i, g * TILE : (g + 1) * TILE, :] = x[
                            i * TILE : (i + 1) * TILE, g * head_dim : (g + 1) * head_dim
                        ]
            kv_out[head, part * rows : (part + 1) * rows, :] = moved(km, ko)


def sort_tokens(after, metas, slot, tiles, q, c, kv):
    heads, n, width = q[0].shape
    head_dim = kv[0].shape[2] // 2
    groups = width // head_dim
    operands = (slot, *q, *c, *kv)
    rows = held((heads, tiles, groups * TILE, head_dim), jnp.bfloat16)
    return pl.pallas_call(
        sort_kernel,
        grid=(heads,),
        in_specs=[ANY]
        + [pl.BlockSpec(memory_space=pltpu.SMEM) for x in metas]
        + [HELD for x in operands],
        out_specs=[HELD, HELD, HELD],
        out_shape=[rows, rows, held((heads, tiles * TILE, 2 * head_dim), jnp.bfloat16)],
        compiler_params=PARAMS,
        cost_estimate=QUICK,
        name="sort_tokens",
    )(after, *metas, *map(hold, operands))


def attend_tile(q, c, own_kv, table, turned, mask):
    head_dim = q.shape[1]
    factor = head_dim ** (-0.5) * math.log2(math.e)
    own_value = own_kv[:, head_dim:]
    own = pick_own(mask, nt(own_kv[:, :head_dim], q))
    score = nt(table[0], q)
    top = jnp.maximum(jnp.max(score, axis=0, keepdims=True), own) * factor
    e = jnp.exp2(score * factor - top)
    own_e = jnp.exp2(own * factor - top)
    inverse = 1.0 / (jnp.sum(e, axis=0, keepdims=True) + own_e)
    prob = e * inverse
    weights = prob.astype(jnp.bfloat16)
    own_w = (own_e * inverse).astype(jnp.bfloat16).astype(jnp.float32)
    dprob = nt(table[1], c)
    delta = jnp.sum(weights.astype(jnp.float32) * dprob, axis=0, keepdims=True)
    delta = delta + own_w * pick_own(mask, nt(own_value, c))
    dweights = (prob * (dprob - delta)).astype(jnp.bfloat16)
    own_part = jnp.where(mask, jnp.broadcast_to(own_w, mask.shape), 0.0)
    out = nn(turned, weights) + tn(own_value, own_part.astype(jnp.bfloat16))
    return weights, dweights, out.T.astype(jnp.bfloat16)


def attend_kernel(js, far, first, n_after, meta, *refs):
    q_ref, c_ref, kv_ref, *refs = refs[n_after:]
    table_refs, (out_ref, *grad_refs) = refs[: len(js)], refs[len(js) :]
    head_dim = q_ref.shape[3]
    rows = q_ref.shape[2]
    n_j = meta.shape[0] // 2
    mask = own_mask(rows)
    out_ref[...] = jnp.zeros_like(out_ref)

    def place(i):
        return pl.ds(pl.multiple_of(i * TILE, TILE), TILE)

    for j, table, grad_ref in zip(js, table_refs, grad_refs):
        start, used = meta[j], meta[n_j + j]

        @pl.loop(0, table.shape[0])
        def _(h):
            head = first + h
            grad = grad_refs[-1] if j == far else grad_ref.at[h]
            grad[...] = jnp.zeros_like(grad)
            pair = table.at[h]
            turned = pair[1].T

            def work(indices):
                done = [
                    attend_tile(
                        q_ref[head, i], c_ref[head, i], kv_ref[head, place(i), :], pair, turned, mask
                    )
                    for i in indices
                ]
                grad[1] += sum(nn(d[0], c_ref[head, i]) for i, d in zip(indices, done))
                grad[0] += sum(nn(d[1], q_ref[head, i]) for i, d in zip(indices, done))
                for i, d in zip(indices, done):
                    for g in range(rows // TILE):
                        out_ref[h, place(i), g * head_dim : (g + 1) * head_dim] = d[2][
                            g * TILE : (g + 1) * TILE
                        ]

            @pl.loop(0, used // 2)
            def _(t):
                work([start + 2 * t, start + 2 * t + 1])

            @pl.when(used % 2 == 1)
            def _():
                work([start + used - 1])

            if j == far:
                grad_ref[h] = grad[...].astype(grad_ref.dtype)


def attend(afters, js, far, first, meta, q, c, kv, tables):
    tiles, rows, head_dim = q.shape[1:]
    count, pair, slots = tables[0].shape[:3]
    outs = [held((count, tiles * TILE, rows // TILE * head_dim), jnp.bfloat16)]
    for j in js:
        kind = jnp.bfloat16 if j == far else jnp.float32
        outs.append(held((count, pair, slots, head_dim), kind))
    operands = (q, c, kv, *tables)
    return pl.pallas_call(
        functools.partial(attend_kernel, js, far if far in js else None, first, len(afters)),
        in_specs=[pl.BlockSpec(memory_space=pltpu.SMEM)]
        + [ANY for x in afters]
        + [HELD for x in operands],
        out_specs=[HELD for x in outs],
        scratch_shapes=[pltpu.VMEM((pair, slots, head_dim), jnp.float32)] if far in js else [],
        out_shape=outs,
        compiler_params=PARAMS,
        cost_estimate=QUICK,
        name="attend",
    )(meta, *afters, *map(hold, operands))


def hop_kernel(*refs):
    partial, acc, out = refs[-3:]
    out[...] = (partial[...] + acc[...].astype(jnp.float32)).astype(out.dtype)


def hop(afters, partial, acc):
    return pl.pallas_call(
        hop_kernel,
        in_specs=[ANY for x in afters] + [HELD, HELD],
        out_specs=HELD,
        out_shape=held(acc.shape, acc.dtype),
        compiler_params=PARAMS,
        cost_estimate=QUICK,
        name="hop",
    )(*afters, hold(partial), hold(acc))


def arrive_kernel(*refs):
    partial, acc, out = refs[-3:]
    half = out.shape[2]
    out[...] = partial[:, :, half:] + acc[:, :, half:].astype(jnp.float32)


def arrive(afters, partial, acc):
    count, pair, slots, head_dim = partial.shape
    return pl.pallas_call(
        arrive_kernel,
        in_specs=[ANY for x in afters] + [HELD, HELD],
        out_specs=HELD,
        out_shape=held((count, pair, slots // 2, head_dim), jnp.float32),
        compiler_params=PARAMS,
        cost_estimate=QUICK,
        name="arrive",
    )(*afters, hold(partial), hold(acc))


def adam_kernel(scale, *refs):
    partial, acc, other, keys, values, first, second = refs[:7]
    new_keys, new_values, new_first, new_second = refs[-4:]
    rows = keys.shape[2]
    at = pl.ds(pl.multiple_of(pl.program_id(0) * rows, rows), rows)
    for i, (param, new) in enumerate(((keys, new_keys), (values, new_values))):
        grad = partial[0, i, at, :] + acc[0, i, at, :].astype(jnp.float32) + other[0, i, at, :]
        if i == 0:
            grad = grad * scale
        moment = 0.9 * first[i, 0, 0] + 0.1 * grad
        square = 0.95 * second[i, 0, 0] + 0.05 * grad * grad
        new_first[i, 0, 0] = moment
        new_second[i, 0, 0] = square
        new[0, 0] = param[0, 0] - 0.02 * moment / (jnp.sqrt(square) + 1e-08)


def adam(head, partial, acc, other, keys, values, first, second, results):
    half, head_dim = keys.shape[2:]
    blocks = 2
    rows = half // blocks
    param = pl.BlockSpec((1, 1, rows, head_dim), lambda i: (0, head, i, 0))
    moment = pl.BlockSpec((2, 1, 1, rows, head_dim), lambda i: (0, 0, head, i, 0))
    arrays = (keys, values, first, second)
    return pl.pallas_call(
        functools.partial(adam_kernel, head_dim ** (-0.5)),
        grid=(blocks,),
        in_specs=[HELD, HELD, HELD, param, param, moment, moment] + [ANY for x in results],
        out_specs=[param, param, moment, moment],
        out_shape=[jax.ShapeDtypeStruct(x.shape, x.dtype) for x in arrays],
        input_output_aliases={7 + i: i for i in range(len(results))},
        compiler_params=PARAMS,
        cost_estimate=QUICK,
        name="adam",
    )(hold(partial), hold(acc), hold(other), *arrays, *results)


def unsort_kernel(after, slot_ref, *refs):
    sources, (mine, other) = refs[:-2], refs[-2:]
    heads, n = mine.shape[:2]
    index = lax.broadcasted_iota(jnp.int32, (n, sources[0].shape[1]), 1)
    for h in range(heads):
        rows = sources[2 * h][0] + sources[2 * h + 1][0]
        slot = jnp.broadcast_to(slot_ref[h].astype(jnp.float32), (8, 2 * n)).T[:, :1]
        for half, out in enumerate((mine, other)):
            one = (index == slot[half * n : (half + 1) * n].astype(jnp.int32)).astype(jnp.bfloat16)
            out[h] = nn(one, rows).astype(jnp.bfloat16)


def unsort(after, slot, sources):
    heads, n = slot.shape[0], slot.shape[2] // 2
    out = held((heads, n, sources[0].shape[2]), jnp.bfloat16)
    return pl.pallas_call(
        unsort_kernel,
        in_specs=[ANY, HELD] + [HELD for x in sources],
        out_specs=[HELD, HELD],
        out_shape=[out, out],
        compiler_params=PARAMS,
        cost_estimate=QUICK,
        name="unsort_answers",
    )(after, hold(slot), *map(hold, sources))


def swap(x):
    return lax.ppermute(x, "rep", [(0, 1), (1, 0)])


def end_core(side, distance, unit):
    return side ^ ((unit + distance + 1) & 1)


def outward(n, step, unit):
    right = [(2 * z, 2 * z + 2) for z in range(step - 1, n - 2)]
    right.append((2 * n - 4, 2 * n - 2 + end_core(0, step, unit)))
    left = [(2 * z + 1, 2 * z - 1) for z in range(2, n - step + 1)]
    left.append((3, end_core(1, step, unit)))
    return right + left


def homeward(n, distance, unit):
    left = [(2 * z, 2 * z - 2) for z in range(distance, n - 1)]
    left.append((2 * n - 2 + end_core(0, distance, unit), 2 * n - 4))
    right = [(2 * z + 1, 2 * z + 3) for z in range(1, n - distance)]
    right.append((end_core(1, distance, unit), 3))
    return left + right


def routes(tables, table_owner, n_owner, unit):
    count = tables.shape[0]
    z, rep = lax.axis_index("owner"), lax.axis_index("rep")
    hit = tables == jnp.arange(table_owner.shape[0], dtype=jnp.int32)[None, :]
    dest = jnp.sum(jnp.where(hit, table_owner[None, :], 0), axis=1, keepdims=True, dtype=jnp.int32)
    js = jnp.arange(n_owner, dtype=jnp.int32)[None, :]
    home = (2 * z >= n_owner).astype(jnp.int32)
    core = jnp.where(dest == z, home, (dest > z).astype(jnp.int32))
    away = jnp.abs(dest - z)
    at_end = (z == 0) | (z == n_owner - 1)
    core = jnp.where(at_end, end_core((z == 0).astype(jnp.int32), away, unit), core)
    asked = (away == js) & (core == rep)
    member = asked.astype(jnp.bfloat16)
    row = lax.broadcasted_iota(jnp.int32, (count, count), 0)
    column = lax.broadcasted_iota(jnp.int32, (count, count), 1)
    rank = jnp.dot(
        (column < row).astype(jnp.bfloat16), member, preferred_element_type=jnp.float32
    ).astype(jnp.int32)
    number = jnp.sum(asked.astype(jnp.int32), axis=0)
    used = (number + TILE - 1) // TILE
    start = jnp.sum(jnp.where(js < js.T, used[None, :], 0), axis=1)
    slot = jnp.sum(jnp.where(asked, start[None, :] * TILE + rank + 1, 0), axis=1) - 1
    return slot, jnp.concatenate([start, used]).astype(jnp.int32)


def move_tables(
    queries,
    cotangent,
    own_kv,
    tables,
    table_owner,
    cache_keys,
    cache_values,
    first_moment,
    second_moment,
):
    n_owner = lax.axis_size("owner")
    heads = queries.shape[1]
    both = ("owner", "rep")
    tiles = -(-(2 * queries.shape[0] // TILE + n_owner - 1) // SORTED) * SORTED
    far = n_owner - 1

    mine = round_table(cache_keys, cache_values)
    mine, queries, cotangent, own_kv = lax.optimization_barrier(
        (mine, queries, cotangent, own_kv)
    )
    units = [{"got": [table]} for table in join(mine, swap(mine))]

    def send(turn, after):
        for u, unit in enumerate(units):
            step = turn - u + 1
            if 1 <= step < n_owner:
                if turn > 1:
                    unit["got"][-1] = tie(unit["got"][-1], after)
                unit["got"].append(
                    lax.ppermute(unit["got"][-1], both, outward(n_owner, step, u % 2))
                )

    def by_head(x):
        mine = jnp.transpose(x, (1, 0, 2))
        return mine, swap(mine)

    asked = jnp.concatenate([tables, swap(tables)], axis=0)
    slots, metas = zip(*(routes(asked, table_owner, n_owner, unit) for unit in (0, 1)))
    slot = jnp.stack([slots[u % 2] for u in range(heads)])[:, None, :]
    send(0, None)
    send(1, None)
    q, c, kv = sort_tokens(
        units[0]["got"][1], metas, slot, tiles, by_head(queries), by_head(cotangent), by_head(own_kv)
    )

    for turn in range(2, far):
        send(turn, kv)

    order = []
    for u in range(heads):
        order.append((2 * u, u, "near", 0))
        order.append((min(2 * u + 3, 2 * heads), u, "far", 0))
        order.append((2 * u + 5.1, u, "hop", far - 1))
        order += [(2 * u + 7.1 + 2 * (k - 2), u, "hop", far - k) for k in range(2, far)]
        order.append((2 * u + 9.2, u, "arrive", 0))

    after = kv
    results = before = ()
    for _, u, what, j in sorted(order):
        unit = units[u]
        if what in ("near", "far"):
            js = tuple(range(far - 1)) if what == "near" else (far - 1, far)
            out, *parts = attend(
                [after], js, far, u, metas[u % 2], q, c, kv, [unit["got"][j] for j in js]
            )
            after = out
            unit[what] = out
            unit.update(zip(js, parts))
            if what == "near":
                send(u + far, after)
            if what == "far":
                unit["acc"] = lax.ppermute(unit[far], both, homeward(n_owner, far, u % 2))
        if what == "hop":
            after = hop([after], unit[j], unit["acc"])
            unit["acc"] = lax.ppermute(after, both, homeward(n_owner, j, u % 2))
            if u == heads - 1 and j == far - 1:
                mine, other = unsort(
                    after, slot, [x[what] for x in units for what in ("near", "far")]
                )
                attended = jnp.transpose(mine + swap(other), (1, 0, 2))
        if what == "arrive":
            last = [outside(attended), outside(before[0])] if u == heads - 1 else []
            after = arrive([after] + last, unit[0], unit["acc"])
            before = results
            results = adam(
                u,
                unit[0],
                unit["acc"],
                swap(after),
                cache_keys,
                cache_values,
                first_moment,
                second_moment,
                results,
            )
    return (attended, *results)


def route_tokens(
    queries,
    cotangent,
    own_kv,
    tables,
    table_owner,
    cache_keys,
    cache_values,
    first_moment,
    second_moment,
):
    n_owner = lax.axis_size("owner")
    q_dev = queries.shape[0]
    heads = queries.shape[1]
    width = queries.shape[2]
    head_dim = own_kv.shape[2] // 2
    groups = width // head_dim
    cap = 2 * q_dev // n_owner
    scale = head_dim ** (-0.5)
    table_hit = tables == jnp.arange(table_owner.shape[0], dtype=jnp.int32)[None, :]
    dest = jnp.sum(jnp.where(table_hit, table_owner[None, :], 0), axis=1, dtype=jnp.int32)
    dest_hit = (dest[:, None] == jnp.arange(n_owner, dtype=jnp.int32)[None, :]).astype(jnp.int32)
    rank = jnp.sum(
        (jnp.cumsum(dest_hit, axis=0, dtype=jnp.int32) - dest_hit) * dest_hit,
        axis=1,
        dtype=jnp.int32,
    )
    place = dest * cap + rank

    def pack(x):
        return jnp.zeros((n_owner * cap,) + x.shape[1:], x.dtype).at[place].set(x)

    sent = (
        lax.all_to_all(pack(queries), "owner", split_axis=0, concat_axis=0, tiled=True),
        lax.all_to_all(pack(cotangent), "owner", split_axis=0, concat_axis=0, tiled=True),
        lax.all_to_all(pack(own_kv), "owner", split_axis=0, concat_axis=0, tiled=True),
    )
    key_half = cache_keys[0].astype(jnp.bfloat16)
    val_half = cache_values[0].astype(jnp.bfloat16)
    q_rows, c_rows, kv_rows = sent
    key_use, val_use = (
        lax.all_gather(key_half, "rep", axis=1, tiled=True),
        lax.all_gather(val_half, "rep", axis=1, tiled=True),
    )
    count = q_rows.shape[0]
    block = 512
    n_blocks = count // block
    q_four = q_rows.reshape(count, heads, groups, head_dim)
    c_four = c_rows.reshape(count, heads, groups, head_dim)
    kself = kv_rows[:, :, :head_dim]
    vself = kv_rows[:, :, head_dim:].astype(jnp.float32)
    q_blocks = q_four.reshape(n_blocks, block, heads, groups, head_dim)
    c_blocks = c_four.reshape(n_blocks, block, heads, groups, head_dim)

    def scores_of(q_block):
        return (
            jnp.einsum("nkgd,ksd->nkgs", q_block, key_use, preferred_element_type=jnp.float32)
            * scale
        )

    def stats(q_block):
        score = scores_of(q_block)
        local_top = jnp.max(score, axis=-1)
        return (local_top, jnp.sum(jnp.exp(score - local_top[..., None]), axis=-1))

    local_top, local_total = lax.map(stats, q_blocks)
    local_top = local_top.reshape(count, heads, groups)
    local_total = local_total.reshape(count, heads, groups)
    own = jnp.einsum("nkgd,nkd->nkg", q_four, kself, preferred_element_type=jnp.float32) * scale
    top = jnp.maximum(local_top, own)
    self_exp = jnp.exp(own - top)
    total = local_total * jnp.exp(local_top - top) + self_exp
    self_weight = (self_exp / total).astype(jnp.bfloat16).astype(jnp.float32)
    top_blocks = top.reshape(n_blocks, block, heads, groups)
    total_blocks = total.reshape(n_blocks, block, heads, groups)

    def weighted(args):
        q_block, top_block, total_block = args
        prob = jnp.exp(scores_of(q_block) - top_block[..., None]) / total_block[..., None]
        return jnp.einsum(
            "nkgs,ksd->nkgd", prob.astype(jnp.bfloat16), val_use, preferred_element_type=jnp.float32
        )

    out_part = lax.map(weighted, (q_blocks, top_blocks, total_blocks)).reshape(
        count, heads, groups, head_dim
    )
    out = out_part + self_weight[..., None] * vself[:, :, None, :]
    delta = jnp.sum(c_four.astype(jnp.float32) * out, axis=-1)
    delta_blocks = delta.reshape(n_blocks, block, heads, groups)

    def backward(carry, args):
        grad_keys, grad_values = carry
        q_block, c_block, top_block, total_block, delta_block = args
        prob = jnp.exp(scores_of(q_block) - top_block[..., None]) / total_block[..., None]
        weights = prob.astype(jnp.bfloat16)
        dprob = jnp.einsum("nkgd,ksd->nkgs", c_block, val_use, preferred_element_type=jnp.float32)
        dweights = (prob * (dprob - delta_block[..., None])).astype(jnp.bfloat16)
        grad_keys = grad_keys + jnp.einsum(
            "nkgs,nkgd->ksd", dweights, q_block, preferred_element_type=jnp.float32
        )
        grad_values = grad_values + jnp.einsum(
            "nkgs,nkgd->ksd", weights, c_block, preferred_element_type=jnp.float32
        )
        return ((grad_keys, grad_values), None)

    zeros_grad = jnp.zeros(key_use.shape, jnp.float32)
    (grad_keys, grad_values), unused = lax.scan(
        backward,
        (zeros_grad, zeros_grad),
        (q_blocks, c_blocks, top_blocks, total_blocks, delta_blocks),
    )
    grad_keys = grad_keys * scale
    answer_rows = out.astype(jnp.bfloat16).reshape(count, heads, width)
    grad_keys, grad_values = (
        lax.psum_scatter(grad_keys, "rep", scatter_dimension=1, tiled=True),
        lax.psum_scatter(grad_values, "rep", scatter_dimension=1, tiled=True),
    )
    returned = lax.all_to_all(answer_rows, "owner", split_axis=0, concat_axis=0, tiled=True)
    attended = returned[place]
    grad = jnp.stack([grad_keys, grad_values])[:, None]
    new_first = 0.9 * first_moment + 0.1 * grad
    new_second = 0.95 * second_moment + 0.05 * grad * grad
    params = jnp.stack([cache_keys, cache_values])
    updated = params - 0.02 * new_first / (jnp.sqrt(new_second) + 1e-08)
    return (attended, updated[0], updated[1], new_first, new_second)


def per_device(*args):
    cap = 2 * args[0].shape[0] // lax.axis_size("owner")
    return move_tables(*args) if cap >= TILE else route_tokens(*args)


def solution(mesh):
    in_specs = (
        P(("groups", "owner", "rep"), "head", None),
        P(("groups", "owner", "rep"), "head", None),
        P(("groups", "owner", "rep"), "head", None),
        P(("groups", "owner", "rep"), None),
        P("groups"),
        P(("groups", "owner"), "head", "rep", None),
        P(("groups", "owner"), "head", "rep", None),
        P(None, ("groups", "owner"), "head", "rep", None),
        P(None, ("groups", "owner"), "head", "rep", None),
    )
    out_specs = (
        P(("groups", "owner", "rep"), "head", None),
        P(("groups", "owner"), "head", "rep", None),
        P(("groups", "owner"), "head", "rep", None),
        P(None, ("groups", "owner"), "head", "rep", None),
        P(None, ("groups", "owner"), "head", "rep", None),
    )
    return jax.shard_map(
        per_device, mesh=mesh, in_specs=in_specs, out_specs=out_specs, check_vma=False
    )
```
